32 devices in a mesh: dp: 8 (over z, core), expert: 4 (over y, x).
Axes of the slice: x: 2, y: 2, z: 4, core: 2. Of those that a mesh axis runs over, the one named last changes fastest.
Arguments:
- tokens: bfloat16 [8192, 1024], P(('dp', 'expert')), may hold values from -6 to 6
- cotangent: bfloat16 [8192, 1024], P(('dp', 'expert')), may hold values from -6 to 6
- route_logits: float32 [8192, 2], P(('dp', 'expert')), may hold values from -6 to 6
- expert_ids: int32 [8192, 2], P(('dp', 'expert')), may hold values from 0 to 7, as said below
- slot_pos: int32 [8192, 2], P(('dp', 'expert')), may hold values from 0 to 127, as said below
- w_in: bfloat16 [8, 1024, 1536], P('expert'), may hold values from -0.1875 to 0.1875
- w_down: bfloat16 [8, 768, 1024], P('expert'), may hold values from -0.21875 to 0.21875
Outputs:
- input_grad: bfloat16 [8192, 1024], P(('dp', 'expert'))
- grad_in: float32 [8, 1024, 1536], P('expert', 'dp')
- grad_down: float32 [8, 768, 1024], P('expert', 'dp')
The draws below stay inside these ranges and needn't reach their ends.
Inputs may be any that keep to these rules, and one draw needn't show every extreme that they name: `expert_ids`: each row names 2 different experts. Within each aligned block of 256 rows (the tokens of one device) no expert is named more than 128 times, and one expert, the same in all blocks, is named exactly 128 times in every block. `slot_pos`: within each aligned block of 256 rows, entries whose matching expert_ids entries name the same expert are distinct.
All inputs are finite; a program needn't handle non-finite values.
Results may differ from the reference program's by a relative error of at most 0.02.
Values may be sent and summed in bfloat16 or wider, within the bound.
No kernel may reach another device: no remote copies, remote signals or barrier semaphores. Data moves between devices by JAX's collectives and lax.ppermute only.
A program may use at most 128 MiB of HBM per device.

```python
import jax
import jax.numpy as jnp
from jax import lax

D = 1024
FF = 768
TOP = 2
TOK_DEV = 256
EXPERTS = 8
CAP = 128
TOKENS = 8192
N_DP = 8
N_EXPERT = 4


def routing_tables(key):
    blocks = TOKENS // TOK_DEV
    favored = jax.random.randint(jax.random.fold_in(key, 7), (), 0, EXPERTS)
    labels = jnp.arange(EXPERTS, dtype=jnp.int32)
    is_full = labels == favored
    positions = jnp.arange(TOP * TOK_DEV, dtype=jnp.int32)
    remainder = TOP * TOK_DEV - CAP

    def shuffled(slot_key):
        return jax.random.permutation(slot_key, CAP).astype(jnp.int32)

    def one_block(index):
        block_key = jax.random.fold_in(jax.random.fold_in(key, 11), index)
        key_weight, key_order, key_slots, key_tokens = jax.random.split(block_key, 4)
        weights = jnp.where(is_full, 0, jax.random.randint(key_weight, (EXPERTS,), 2, 5)).astype(jnp.int32)
        shares = (weights * remainder // jnp.sum(weights)).astype(jnp.int32)
        leftover = remainder - jnp.sum(shares)
        order = jax.random.permutation(key_order, EXPERTS).astype(jnp.int32)
        ranking = jnp.zeros((EXPERTS,), jnp.int32).at[order].set(labels)
        full_rank = jnp.sum(jnp.where(is_full, ranking, 0))
        other_rank = ranking - (ranking > full_rank).astype(jnp.int32)
        extra = jnp.logical_and(jnp.logical_not(is_full), other_rank < leftover).astype(jnp.int32)
        counts = jnp.where(is_full, CAP, shares + extra).astype(jnp.int32)
        ends = jnp.cumsum(counts).astype(jnp.int32)
        starts = ends - counts
        label_at = jnp.sum((ends[None, :] <= positions[:, None]).astype(jnp.int32), axis=1)
        within = positions - starts[label_at]
        tables = jax.vmap(shuffled)(jax.random.split(key_slots, EXPERTS))
        slot_at = tables[label_at, within]
        ids_block = label_at.reshape(TOP, TOK_DEV).T
        slots_block = slot_at.reshape(TOP, TOK_DEV).T
        mixing = jax.random.permutation(key_tokens, TOK_DEV)
        return (ids_block[mixing], slots_block[mixing])
    chosen, places = lax.map(one_block, jnp.arange(blocks, dtype=jnp.int32))
    return (chosen.reshape(TOKENS, TOP).astype(jnp.int32), places.reshape(TOKENS, TOP).astype(jnp.int32))


def draw_expert_ids(key, part):
    return routing_tables(jax.random.fold_in(key, 3))[0]


def draw_slot_pos(key, part):
    return routing_tables(jax.random.fold_in(key, 3))[1]


def block_levels(key, dims, cuts, low, top_value):
    gain = 1.0
    for dim, parts in cuts:
        heights = jax.random.uniform(jax.random.fold_in(jax.random.fold_in(key, 6), dim), (parts,), jnp.float32, low / len(cuts), top_value / len(cuts))
        gain = gain * jnp.repeat(jnp.exp(heights), dims[dim] // parts).reshape((-1,) + (1,) * (len(dims) - 1 - dim))
    return gain


def normal_values(stream_key, extent, spread, limit, cuts=(), kind=jnp.bfloat16):
    values = spread * jax.random.normal(stream_key, extent, jnp.float32)
    if cuts:
        values = values * block_levels(stream_key, extent, cuts, -0.22, 0.18)
    return jnp.clip(values, -limit, limit).astype(kind)


def setup_inputs(seed: int = 0) -> dict:
    streams_of = jax.random.split(jax.random.key(seed), 8)
    tokens = normal_values(streams_of[0], (TOKENS, D), 1.0, 6.0, ((0, 32),))
    cotangent = normal_values(streams_of[1], (TOKENS, D), 1.0, 6.0, ((0, 32),))
    route_logits = normal_values(streams_of[2], (TOKENS, TOP), 1.5, 6.0, ((0, 32),), jnp.float32)
    expert_ids = draw_expert_ids(jax.random.fold_in(streams_of[7], 71), 0)
    slot_pos = draw_slot_pos(jax.random.fold_in(streams_of[7], 71), 0)
    w_in = normal_values(streams_of[5], (EXPERTS, D, 2 * FF), D ** -0.5, 0.1875, ((0, 4),))
    w_down = normal_values(streams_of[6], (EXPERTS, FF, D), FF ** -0.5, 0.21875, ((0, 4),))
    return dict(tokens=tokens, cotangent=cotangent, route_logits=route_logits, expert_ids=expert_ids, slot_pos=slot_pos, w_in=w_in, w_down=w_down)


def reference(tokens, cotangent, route_logits, expert_ids, slot_pos, w_in, w_down):
    group_rows = N_EXPERT * TOK_DEV
    slots_all = N_EXPERT * CAP
    w_in_wide = w_in.astype(jnp.float32)
    w_down_wide = w_down.astype(jnp.float32)
    source = (jnp.arange(group_rows, dtype=jnp.int32) // TOK_DEV) * CAP

    def one_group(carry, group):
        sum_in, sum_down = carry
        inputs, cotan, logits, chosen, places = group
        first = jax.nn.sigmoid(logits[:, 0] - logits[:, 1])
        combine = jnp.stack([first, 1.0 - first], axis=1)
        scaled = (combine[:, :, None] * cotan[:, None, :].astype(jnp.float32)).astype(jnp.bfloat16)
        scaled = lax.optimization_barrier(scaled)
        destination = (chosen.astype(jnp.int32) * slots_all + source[:, None] + places.astype(jnp.int32)).reshape(-1)
        empty = jnp.zeros((EXPERTS * slots_all, D), jnp.bfloat16)
        repeated = jnp.broadcast_to(inputs[:, None, :], (group_rows, TOP, D)).reshape(-1, D)
        input_slots = empty.at[destination].set(repeated).reshape(EXPERTS, slots_all, D).astype(jnp.float32)
        cotangent_slots = empty.at[destination].set(scaled.reshape(-1, D)).reshape(EXPERTS, slots_all, D).astype(jnp.float32)
        gate_up = jnp.einsum("esd,edf->esf", input_slots, w_in_wide)
        gate = gate_up[:, :, :FF]
        upper = gate_up[:, :, FF:]
        sigmoid_gate = jax.nn.sigmoid(gate)
        activated = gate * sigmoid_gate
        hidden = lax.optimization_barrier((activated * upper).astype(jnp.bfloat16)).astype(jnp.float32)
        grad_hidden = jnp.einsum("esd,efd->esf", cotangent_slots, w_down_wide)
        grad_gate = grad_hidden * upper * sigmoid_gate * (1.0 + gate * (1.0 - sigmoid_gate))
        grad_up = grad_hidden * activated
        grad_pair = jnp.concatenate([grad_gate, grad_up], axis=2).astype(jnp.bfloat16)
        grad_pair = lax.optimization_barrier(grad_pair).astype(jnp.float32)
        term_down = jnp.einsum("esf,esd->efd", hidden, cotangent_slots)
        term_in = jnp.einsum("esd,esf->edf", input_slots, grad_pair)
        returned = jnp.einsum("esf,edf->esd", grad_pair, w_in_wide).astype(jnp.bfloat16)
        returned = lax.optimization_barrier(returned)
        rows = returned.reshape(-1, D)[destination].reshape(group_rows, TOP, D)
        token_grad = jnp.sum(rows.astype(jnp.float32), axis=1).astype(jnp.bfloat16)
        sum_in = sum_in + lax.optimization_barrier(term_in.astype(jnp.bfloat16)).astype(jnp.float32)
        sum_down = sum_down + lax.optimization_barrier(term_down.astype(jnp.bfloat16)).astype(jnp.float32)
        return (sum_in, sum_down), token_grad

    start = (jnp.zeros((EXPERTS, D, 2 * FF), jnp.float32), jnp.zeros((EXPERTS, FF, D), jnp.float32))
    grouped = (
        tokens.reshape(N_DP, group_rows, D),
        cotangent.reshape(N_DP, group_rows, D),
        route_logits.reshape(N_DP, group_rows, TOP),
        expert_ids.reshape(N_DP, group_rows, TOP),
        slot_pos.reshape(N_DP, group_rows, TOP),
    )
    (grad_in, grad_down), token_grads = lax.scan(one_group, start, grouped)
    return token_grads.reshape(TOKENS, D), grad_in, grad_down
```

```python
import functools

import jax
import jax.numpy as jnp
from jax import lax
from jax.experimental import pallas as pl
from jax.experimental.pallas import tpu as pltpu
from jax.sharding import PartitionSpec as P

TOP = 2
BF = jnp.bfloat16
F32 = jnp.float32
VMEM_BYTES = 40 * 1024 * 1024


def dot(a, b):
    return jnp.dot(a, b, preferred_element_type=F32)


def dot_nt(a, b):
    return lax.dot_general(a, b, (((1,), (1,)), ((), ())), preferred_element_type=F32)


def call(body, grid, in_specs, out_specs, out_shape, scratch, flops, moved, *args):
    return pl.pallas_call(
        body,
        out_shape=out_shape,
        grid_spec=pltpu.PrefetchScalarGridSpec(
            num_scalar_prefetch=1,
            grid=grid,
            in_specs=in_specs,
            out_specs=out_specs,
            scratch_shapes=scratch,
        ),
        compiler_params=pltpu.CompilerParams(vmem_limit_bytes=VMEM_BYTES),
        cost_estimate=pl.CostEstimate(flops=flops, bytes_accessed=moved, transcendentals=0),
    )(*args)


def whole(array):
    return pl.BlockSpec(array.shape, lambda e, scal: (0,) * array.ndim)


def per_expert(shape):
    return pl.BlockSpec((1,) + tuple(shape), lambda e, scal: (e,) + (0,) * len(shape))


def load_source(refs, parts, rows):
    blocks = [refs[ref][pl.ds(first, count), :] for ref, first, count in parts]
    return blocks[0] if len(blocks) == 1 else jnp.concatenate(blocks, axis=0)


def forward_body(layout, cap, tile, scal, route, *refs):
    pieces = refs[: layout["pieces"]]
    w_in = refs[layout["pieces"]]
    rows_t, hidden_t, scale_gate, scale_up, onehot, onehot_t, weight = refs[layout["pieces"] + 1 :]
    width = w_in.shape[1]
    ff = w_in.shape[2] // 2
    expert = pl.program_id(0)
    base = (scal[0] + expert * cap).astype(F32)
    tokens = route.shape[2]
    slot = lax.broadcasted_iota(jnp.int32, (cap, tokens), 0).astype(F32) + base
    gathered = []
    for s, parts in enumerate(layout["sources"]):
        first = slot == route[s, 0:1, :]
        second = slot == route[s, 1:2, :]
        hit = jnp.where(jnp.logical_or(first, second), 1.0, 0.0)
        factor = jnp.where(first, route[s, 2:3, :], 0.0) + jnp.where(second, route[s, 3:4, :], 0.0)
        factor = jnp.sum(factor, axis=1, keepdims=True)
        place = pl.ds(s * cap, cap)
        onehot[0, place, :] = hit.astype(BF)
        onehot_t[0, s] = jnp.transpose(hit).astype(BF)
        weight[0, place, :] = jnp.broadcast_to(factor, (cap, 128))
        gathered.append(dot(hit.astype(BF), load_source(pieces, parts, tokens)).astype(BF))
    rows = jnp.concatenate(gathered, axis=0)
    rows_t[0] = jnp.transpose(rows)
    for f in range(0, ff, tile):
        gate = dot(rows, w_in[0, :, pl.ds(f, tile)])
        upper = dot(rows, w_in[0, :, pl.ds(ff + f, tile)])
        sg = jax.nn.sigmoid(gate)
        activated = gate * sg
        hidden_t[0, pl.ds(f, tile), :] = jnp.transpose((activated * upper).astype(BF))
        scale_gate[0, :, pl.ds(f, tile)] = (upper * sg * (1.0 + gate * (1.0 - sg))).astype(BF)
        scale_up[0, :, pl.ds(f, tile)] = activated.astype(BF)


def cotangent_body(layout, cap, nz, start, last, scal, onehot, weight, hidden_t, *refs):
    refs = list(refs)
    pieces = [refs.pop(0) for _ in range(layout["pieces"])]
    w_down = refs.pop(0)
    if not start:
        before = refs.pop(0)
    if last:
        scale_gate, scale_up = refs.pop(0), refs.pop(0)
    give, keep, after = refs
    expert = pl.program_id(0)
    slots = []
    for s, parts in enumerate(layout["sources"]):
        place = pl.ds(s * cap, cap)
        block = load_source(pieces, parts, onehot.shape[2])
        factor = weight[0, place, 0:1]
        slots.append((dot(onehot[0, place, :], block) * factor).astype(BF))
    slots = jnp.concatenate(slots, axis=0)
    part = give.shape[2]
    for out, offset in ((give, scal[2]), (keep, scal[1])):
        left = []
        for t in range(nz):
            shard = scal[3 + t + nz * expert]
            left.append(hidden_t[0, pl.ds(pl.multiple_of((2 * shard + offset) * part, 16), part), :])
        result = dot(jnp.concatenate(left, axis=0), slots).astype(BF)
        for t in range(nz):
            out[t, 0] = result[t * part : (t + 1) * part]
    grad_hidden = dot_nt(slots, w_down[0])
    if not start:
        grad_hidden = grad_hidden + before[0]
    if last:
        ff = scale_gate.shape[2]
        after[0, :, pl.ds(0, ff)] = (grad_hidden * scale_gate[0].astype(F32)).astype(BF)
        after[0, :, pl.ds(ff, ff)] = (grad_hidden * scale_up[0].astype(F32)).astype(BF)
    else:
        after[0] = grad_hidden


def input_weight_body(nz, steps, scal, rows_t, pair, give, keep):
    expert = pl.program_id(0)
    part = give.shape[2]
    left = []
    for t in steps:
        shard = scal[3 + t + nz * expert]
        for offset in (scal[2], scal[1]):
            left.append(rows_t[0, pl.ds(pl.multiple_of((2 * shard + offset) * part, 16), part), :])
    left = jnp.concatenate(left, axis=0)
    for f in range(0, pair.shape[2], 256):
        result = dot(left, pair[0, :, pl.ds(f, 256)]).astype(BF)
        for t in range(len(steps)):
            give[t, 0, :, pl.ds(f, 256)] = result[2 * t * part : (2 * t + 1) * part]
            keep[t, 0, :, pl.ds(f, 256)] = result[(2 * t + 1) * part : (2 * t + 2) * part]


def returned_body(outputs, cap, experts, scal, pair, w_in, onehot_t, *refs):
    outs, total = refs[:-1], refs[-1]
    expert = pl.program_id(0)
    sources = onehot_t.shape[1]
    width = w_in.shape[1]
    for n in range(0, width, 256):
        returned = dot_nt(pair[0], w_in[0, pl.ds(n, 256), :]).astype(BF)
        for s in range(sources):
            share = dot(onehot_t[0, s], returned[s * cap : (s + 1) * cap])

            @pl.when(expert == 0)
            def _():
                total[s, :, pl.ds(n, 256)] = share

            @pl.when(expert > 0)
            def _():
                total[s, :, pl.ds(n, 256)] += share

    @pl.when(expert == experts - 1)
    def _():
        for out, index, s, first, count in outputs:
            outs[out][index] = total[s, pl.ds(first, count), :].astype(BF)


def gather_blocks(block, n):
    rows = block.shape[0]
    if n != 4:
        everything = lax.all_gather(block, "expert", tiled=True)
        return [everything], [[(0, s * rows, rows)] for s in range(n)]
    half = rows // 2
    low, high = block[:half], block[half:]
    across_x = functools.partial(lax.ppermute, axis_name="expert", perm=[(i, i ^ 1) for i in range(4)])
    across_y = functools.partial(lax.ppermute, axis_name="expert", perm=[(i, i ^ 2) for i in range(4)])
    x_low, y_high = across_x(low), across_y(high)
    x_high, y_low = across_x(high), across_y(low)
    d_low, d_high = across_y(x_low), across_x(y_high)
    pieces = [block, x_low, x_high, y_low, y_high, d_low, d_high]
    sources = [[(0, 0, rows)]] + [[(k, 0, half), (k + 1, 0, half)] for k in (1, 3, 5)]
    return pieces, sources


def gather_routes(route, n):
    if n != 4:
        return lax.all_gather(route, "expert")
    others = [lax.ppermute(route, "expert", [(i, i ^ k) for i in range(4)]) for k in (1, 2, 3)]
    return jnp.stack([route] + others)


def add(*terms):
    return functools.reduce(jnp.add, [t.astype(F32) for t in terms])


def ring_sum(own, nz, experts):
    half = experts // 2
    up = [(i, (i + 2) % (2 * nz)) for i in range(2 * nz)]
    down = [(j, i) for i, j in up]
    held = [None, None]
    for t in range(nz):
        sums = []
        for way, chosen in enumerate((slice(0, half), slice(half, experts))):
            terms = [x[chosen] for x in own(t)]
            if held[way] is not None:
                terms.append(held[way])
            sums.append(add(*terms))
        if t == nz - 1:
            return jnp.concatenate(sums, axis=0)
        held = [
            lax.ppermute(total.astype(BF), "dp", perm) for total, perm in zip(sums, (up, down))
        ]


def per_device(column_parts, tokens, cotangent, route_logits, expert_ids, slot_pos, w_in, w_down):
    token_count, width = tokens.shape
    experts, ff = w_down.shape[:2]
    n = lax.axis_size("expert")
    ndp = lax.axis_size("dp")
    nz = ndp // 2
    cap = 2 * TOP * token_count // (experts * n)
    slots = n * cap
    place = lax.axis_index("dp")
    z, core = place // 2, place % 2
    swap = functools.partial(
        lax.ppermute, axis_name="dp", perm=[(i, i ^ 1) for i in range(ndp)]
    )

    token_pieces, token_sources = gather_blocks(tokens, n)
    first = jax.nn.sigmoid(route_logits[:, 0] - route_logits[:, 1])
    destination = (expert_ids * cap + slot_pos).astype(F32)
    route = jnp.stack([destination[:, 0], destination[:, 1], first, 1.0 - first])
    route = gather_routes(jnp.concatenate([route, jnp.zeros_like(route)]), n)
    columns = width // column_parts
    cot_parts = [
        gather_blocks(cotangent[:, k * columns : (k + 1) * columns], n) for k in range(column_parts)
    ]

    steps = jnp.arange(1, nz + 1)
    ups = (z - steps) % nz
    downs = (z + steps) % nz
    scal = jnp.concatenate(
        [jnp.stack([lax.axis_index("expert") * experts * cap, core, 1 - core])]
        + [ups] * (experts // 2)
        + [downs] * (experts - experts // 2)
    ).astype(jnp.int32)

    s3 = lambda *shape: jax.ShapeDtypeStruct(shape, BF)
    layout = dict(pieces=len(token_pieces), sources=token_sources)
    macs = experts * slots * width * ff
    rows_t, hidden_t, scale_gate, scale_up, onehot, onehot_t, weight = call(
        functools.partial(forward_body, layout, cap, 256),
        (experts,),
        [whole(route)] + [whole(p) for p in token_pieces] + [per_expert(w_in.shape[1:])],
        [
            per_expert((width, slots)),
            per_expert((ff, slots)),
            per_expert((slots, ff)),
            per_expert((slots, ff)),
            per_expert((slots, token_count)),
            per_expert((n, token_count, cap)),
            per_expert((slots, 128)),
        ],
        [
            s3(experts, width, slots),
            s3(experts, ff, slots),
            s3(experts, slots, ff),
            s3(experts, slots, ff),
            s3(experts, slots, token_count),
            s3(experts, n, token_count, cap),
            jax.ShapeDtypeStruct((experts, slots, 128), F32),
        ],
        [],
        4 * macs,
        16 << 20,
        scal,
        route,
        *token_pieces,
        w_in,
    )

    down_rows = ff // ndp
    in_rows = width // ndp
    after = None
    downs_given = []
    for k, (pieces, sources) in enumerate(cot_parts):
        start, last = k == 0, k == column_parts - 1
        layout = dict(pieces=len(pieces), sources=sources)
        piece_of = pl.BlockSpec((1, ff, columns), functools.partial(lambda k, e, scal: (e, 0, k), k))
        stepwise = pl.BlockSpec((nz, 1, down_rows, columns), lambda e, scal: (0, e, 0, 0))
        extra = [] if start else [after]
        if last:
            extra += [scale_gate, scale_up]
        after_shape = (experts, slots, 2 * ff) if last else (experts, slots, ff)
        give, keep, after = call(
            functools.partial(cotangent_body, layout, cap, nz, start, last),
            (experts,),
            [per_expert(onehot.shape[1:]), per_expert(weight.shape[1:]), per_expert(hidden_t.shape[1:])]
            + [whole(p) for p in pieces]
            + [piece_of]
            + [per_expert(x.shape[1:]) for x in extra],
            [stepwise, stepwise, per_expert(after_shape[1:])],
            [s3(nz, experts, down_rows, columns)] * 2
            + [jax.ShapeDtypeStruct(after_shape, BF if last else F32)],
            [],
            4 * macs // column_parts,
            8 << 20,
            scal,
            onehot,
            weight,
            hidden_t,
            *pieces,
            w_down,
            *extra,
        )
        downs_given.append((keep, swap(give)))
    pair = after

    ins_given = []
    for chosen in ((0,), tuple(range(1, nz))):
        stepwise = pl.BlockSpec((len(chosen), 1, in_rows, 2 * ff), lambda e, scal: (0, e, 0, 0))
        give, keep = call(
            functools.partial(input_weight_body, nz, chosen),
            (experts,),
            [per_expert(rows_t.shape[1:]), per_expert(pair.shape[1:])],
            [stepwise, stepwise],
            [s3(len(chosen), experts, in_rows, 2 * ff)] * 2,
            [],
            4 * macs * len(chosen) // nz,
            8 << 20,
            scal,
            rows_t,
            pair,
        )
        other = swap(give)
        ins_given += [(keep[t], other[t]) for t in range(len(chosen))]

    if n == 4:
        half = token_count // 2
        outputs = [
            (0, 0, 2, 0, half),
            (0, 1, 3, 0, half),
            (1, 0, 1, half, half),
            (1, 1, 3, half, half),
            (2, 0, 0, 0, half),
            (2, 1, 1, 0, half),
            (3, 0, 0, half, half),
            (3, 1, 2, half, half),
        ]
        out_shapes = [s3(2, half, width)] * 4
    else:
        outputs = [(0, s, s, 0, token_count) for s in range(n)]
        out_shapes = [s3(n, token_count, width)]
    shares = call(
        functools.partial(returned_body, outputs, cap, experts),
        (experts,),
        [per_expert(pair.shape[1:]), per_expert(w_in.shape[1:]), per_expert(onehot_t.shape[1:])],
        [whole(x) for x in out_shapes],
        out_shapes,
        [pltpu.VMEM((n, token_count, width), F32)],
        4 * macs,
        16 << 20,
        scal,
        pair,
        w_in,
        onehot_t,
    )
    if n == 4:
        across_x = functools.partial(lax.ppermute, axis_name="expert", perm=[(i, i ^ 1) for i in range(4)])
        across_y = functools.partial(lax.ppermute, axis_name="expert", perm=[(i, i ^ 2) for i in range(4)])
        to_y, to_x, low, high = shares
        from_y, from_x = across_y(to_y), across_x(to_x)
        low_x = across_x(add(low[1], from_y[1]).astype(BF))
        high_y = across_y(add(high[1], from_x[1]).astype(BF))
        input_grad = jnp.concatenate(
            [add(low[0], from_y[0], low_x), add(high[0], from_x[0], high_y)], axis=0
        ).astype(BF)
    else:
        input_grad = lax.psum_scatter(shares[0], "expert", scatter_dimension=0)

    grad_down = jnp.concatenate(
        [ring_sum(lambda t: (keep[t], other[t]), nz, experts) for keep, other in downs_given], axis=2
    )
    grad_in = ring_sum(lambda t: ins_given[t], nz, experts)
    return (input_grad, grad_in, grad_down)


def solution(mesh):
    in_specs = (
        P(("dp", "expert"), None),
        P(("dp", "expert"), None),
        P(("dp", "expert"), None),
        P(("dp", "expert"), None),
        P(("dp", "expert"), None),
        P("expert", None, None),
        P("expert", None, None),
    )
    out_specs = (P(("dp", "expert"), None), P("expert", "dp", None), P("expert", "dp", None))
    return jax.shard_map(
        functools.partial(per_device, 2),
        mesh=mesh,
        in_specs=in_specs,
        out_specs=out_specs,
        check_vma=False,
    )
```

```python
import functools

import jax
import jax.numpy as jnp
from jax import lax
from jax.experimental import pallas as pl
from jax.experimental.pallas import tpu as pltpu
from jax.sharding import PartitionSpec as P

TOP = 2
BF = jnp.bfloat16
F32 = jnp.float32
IN_PARTS = 1


def dot(a, b):
    return jnp.dot(a, b, preferred_element_type=F32)


def dot_nt(a, b):
    return lax.dot_general(a, b, (((1,), (1,)), ((), ())), preferred_element_type=F32)


def bf(*shape):
    return jax.ShapeDtypeStruct(shape, BF)


def whole(array):
    return pl.BlockSpec(array.shape, lambda step, scal: (0,) * len(array.shape))


def of_expert(weights, columns=None, index=0):
    shape = (1, weights.shape[1], columns or weights.shape[2])
    return pl.BlockSpec(shape, lambda step, scal: (scal[0], 0, index))


def call(body, out_shape, flops, limit, scal, *args, specs=None):
    return pl.pallas_call(
        body,
        out_shape=out_shape,
        grid_spec=pltpu.PrefetchScalarGridSpec(
            num_scalar_prefetch=1,
            grid=(1,),
            in_specs=specs or [whole(x) for x in args],
            out_specs=[whole(x) for x in out_shape],
        ),
        compiler_params=pltpu.CompilerParams(vmem_limit_bytes=limit << 20),
        cost_estimate=pl.CostEstimate(flops=flops, bytes_accessed=flops // 1000, transcendentals=0),
    )(scal, *args)


def stack_rows(refs, index):
    return jnp.concatenate([ref[index] for ref in refs], axis=0)


def after(value, *others):
    return lax.optimization_barrier((value, *others))[0]


ROUTE_ROWS = 16


def route_rows(route_logits, expert_ids, slot_pos, width):
    share = jax.nn.sigmoid(route_logits[:, 0] - route_logits[:, 1])
    high = lax.reduce_precision(share, 8, 7)
    middle = lax.reduce_precision(share - high, 8, 7)
    low = share - high - middle
    places = jnp.concatenate(
        [x.astype(BF) for x in (expert_ids[:, 0], expert_ids[:, 1], slot_pos[:, 0], slot_pos[:, 1])]
    )
    shares = jnp.concatenate([x.astype(BF) for x in (high, middle, low)])
    rows = [jnp.pad(x, (0, width - x.shape[0])) for x in (places, shares)]
    return jnp.pad(jnp.stack(rows), ((0, ROUTE_ROWS - 2), (0, 0)))


def slots_body(cap, n, scal, block, *refs):
    outs, back = refs[:-1], refs[-1]
    tokens = back.shape[0]
    route = block[0:2, :].astype(F32)
    row = lambda r, k: route[r : r + 1, k * tokens : (k + 1) * tokens]
    slot = lax.broadcasted_iota(jnp.int32, (cap, tokens), 0)
    slot = jnp.concatenate([slot + scal[2 + j] for j in range(n)], axis=0).astype(F32)
    first = slot == row(0, 0) * cap + row(0, 2)
    second = slot == row(0, 1) * cap + row(0, 3)
    share = row(1, 0) + row(1, 1) + row(1, 2)
    hit = jnp.where(jnp.logical_or(first, second), 1.0, 0.0)
    factor = jnp.where(first, share, 0.0) + jnp.where(second, 1.0 - share, 0.0)
    factor = jnp.sum(factor, axis=1, keepdims=True)
    back[...] = jnp.transpose(hit).astype(BF)
    hit = hit.astype(BF)
    rows = dot(hit, block[pl.ds(ROUTE_ROWS, tokens), :]).astype(BF)
    scaled = (dot(hit, block[pl.ds(ROUTE_ROWS + tokens, tokens), :]) * factor).astype(BF)
    for j, out in enumerate(outs):
        out[0] = rows[j * cap : (j + 1) * cap]
        out[1] = scaled[j * cap : (j + 1) * cap]


def forward_body(tile, scal, *refs):
    *arrived, w_in, rows_t, hidden_t, scale_gate, scale_up = refs
    ff = w_in.shape[2] // 2
    rows = stack_rows(arrived, 0)
    rows_t[...] = jnp.transpose(rows)
    for f in range(0, ff, tile):
        gate = dot(rows, w_in[0, :, pl.ds(f, tile)])
        upper = dot(rows, w_in[0, :, pl.ds(ff + f, tile)])
        sg = jax.nn.sigmoid(gate)
        activated = gate * sg
        hidden_t[pl.ds(f, tile), :] = jnp.transpose((activated * upper).astype(BF))
        scale_gate[:, pl.ds(f, tile)] = (upper * sg * (1.0 + gate * (1.0 - sg))).astype(BF)
        scale_up[:, pl.ds(f, tile)] = activated.astype(BF)


def shard_rows(sources, scal, shards, part):
    taken = []
    for offset in (1 - scal[1], scal[1]):
        for shard in shards:
            start = pl.multiple_of((2 * shard + offset) * part, 16)
            taken.append(jnp.concatenate([x[pl.ds(start, part), :] for x in sources], axis=1))
    return jnp.concatenate(taken, axis=0)


def down_body(n, nz, scal, *refs):
    arrived, (w_down, hidden_a, hidden_b, *scales), outs = refs[: 2 * n], refs[2 * n : 2 * n + 7], refs[2 * n + 7 :]
    give, keep, *pairs = outs
    part = give.shape[1]
    slots = [stack_rows(arrived[:n], 1), stack_rows(arrived[n:], 1)]
    shards = [scal[scal.shape[0] - nz + k] for k in range(nz)]
    left = shard_rows((hidden_a, hidden_b), scal, shards, part)
    result = dot(left, jnp.concatenate(slots, axis=0)).astype(BF)
    for k in range(nz):
        give[k] = result[k * part : (k + 1) * part]
        keep[k] = result[(nz + k) * part : (nz + k + 1) * part]
    for g in range(2):
        grad_hidden = dot_nt(slots[g], w_down[0])
        scale_gate, scale_up = scales[2 * g : 2 * g + 2]
        ff = scale_gate.shape[1]
        pairs[g][:, pl.ds(0, ff)] = (grad_hidden * scale_gate[...].astype(F32)).astype(BF)
        pairs[g][:, pl.ds(ff, ff)] = (grad_hidden * scale_up[...].astype(F32)).astype(BF)


def input_weight_body(first, nz, scal, rows_a, rows_b, pair_a, pair_b, give, keep):
    part, columns = give.shape[1:]
    pair = jnp.concatenate(
        [pair_a[:, pl.ds(first, columns)], pair_b[:, pl.ds(first, columns)]], axis=0
    )
    result = dot(shard_rows((rows_a, rows_b), scal, range(nz), part), pair).astype(BF)
    for k in range(nz):
        give[k] = result[k * part : (k + 1) * part]
        keep[k] = result[(nz + k) * part : (nz + k + 1) * part]


def returned_body(cap, scal, pair_a, pair_b, w_in, *outs):
    for g, pair in enumerate((pair_a, pair_b)):
        returned = dot_nt(pair[...], w_in[0]).astype(BF)
        for j, out in enumerate(outs):
            out[pl.ds(g * cap, cap), :] = returned[j * cap : (j + 1) * cap]


def combine_body(cap, scal, back_a, back_b, *refs):
    arrived, outs = refs[:-2], refs[-2:]
    for g, (back, out) in enumerate(zip((back_a, back_b), outs)):
        rows = jnp.concatenate([x[pl.ds(g * cap, cap), :] for x in arrived], axis=0)
        out[...] = dot(back[...], rows).astype(BF)


def per_device(tokens, cotangent, route_logits, expert_ids, slot_pos, w_in, w_down):
    token_count, width = tokens.shape
    experts, ff = w_down.shape[:2]
    n = lax.axis_size("expert")
    ndp = lax.axis_size("dp")
    nz = ndp // 2
    cap = 2 * TOP * token_count // (experts * n)
    slots = n * cap
    column, place = lax.axis_index("expert"), lax.axis_index("dp")
    z, core = place // 2, place % 2
    expert_of = lambda k: (k ^ (k >> 1)) & 1
    mine = expert_of(z)
    scal = [mine, core]
    scal += [((column ^ j) * experts + mine) * cap for j in range(n)]
    scal += [z ^ k for k in range(nz)]
    scal = jnp.stack(scal).astype(jnp.int32)
    swap_core = lambda x: lax.ppermute(x, "dp", [(i, i ^ 1) for i in range(ndp)])
    along_z = lambda x, k: lax.ppermute(x, "dp", [(i, i ^ (2 * k)) for i in range(ndp)]) if k else x
    across = lambda x, j: lax.ppermute(x, "expert", [(i, i ^ j) for i in range(n)]) if j else x
    macs = 2 * slots * width * ff

    block = jnp.concatenate(
        [route_rows(route_logits, expert_ids, slot_pos, width), tokens, cotangent], axis=0
    )
    arrived, backs = [], []
    for block in (block, along_z(block, 1)):
        *sent, back = call(
            functools.partial(slots_body, cap, n),
            [bf(2, cap, width)] * n + [bf(token_count, slots)],
            macs // 4,
            LIMITS[0],
            scal,
            block,
        )
        arrived += [across(x, j) for j, x in enumerate(sent)]
        backs.append(back)

    forwards = []
    for g in range(2):
        pieces = arrived[g * n : (g + 1) * n]
        forwards.append(
            call(
                functools.partial(forward_body, 256),
                [bf(width, slots), bf(ff, slots), bf(slots, ff), bf(slots, ff)],
                2 * macs,
                LIMITS[1],
                scal,
                *pieces,
                w_in,
                specs=[whole(x) for x in pieces] + [of_expert(w_in)],
            )
        )
    (rows_a, hidden_a, *scales_a), (rows_b, hidden_b, *scales_b) = forwards

    args = arrived + [w_down, hidden_a, hidden_b] + scales_a + scales_b
    specs = [whole(x) for x in args]
    specs[2 * n] = of_expert(w_down)
    *down, pair_a, pair_b = call(
        functools.partial(down_body, n, nz),
        [bf(nz, ff // ndp, width)] * 2 + [bf(slots, 2 * ff)] * 2,
        4 * macs,
        LIMITS[2],
        scal,
        *args,
        specs=specs,
    )
    pairs = (pair_a, pair_b)

    columns = 2 * ff // IN_PARTS
    ins = [
        call(
            functools.partial(input_weight_body, k * columns, nz),
            [bf(nz, width // ndp, columns)] * 2,
            4 * macs // IN_PARTS,
            LIMITS[3],
            scal,
            rows_a,
            rows_b,
            *pairs,
        )
        for k in range(IN_PARTS)
    ]

    def core_sum(give, keep):
        other = swap_core(give)
        return [(keep[k].astype(F32) + other[k].astype(F32)).astype(BF) for k in range(nz)]

    def gather_z(terms):
        return [along_z(x, k) for k, x in enumerate(terms)]

    def over_z(terms):
        same, different = (
            sum(terms[k].astype(F32) for k in range(nz) if expert_of(k) == e) for e in range(2)
        )
        return jnp.where(mine == 0, jnp.stack([same, different]), jnp.stack([different, same]))

    down_terms = gather_z(core_sum(*down))
    grad_down = over_z(down_terms)
    (give, keep) = ins[0]
    total = (keep.astype(F32) + swap_core(give).astype(F32)).astype(BF)
    terms = lax.all_to_all(
        total, "dp", 0, 0, tiled=True, axis_index_groups=[list(range(c, ndp, 2)) for c in range(2)]
    )
    grad_in = jnp.stack(
        [sum(terms[k].astype(F32) for k in range(nz) if expert_of(k) == e) for e in range(experts)]
    )
    sent = call(
        functools.partial(returned_body, cap),
        [bf(2 * cap, width)] * n,
        4 * macs,
        LIMITS[4],
        scal,
        after(pairs[0], total),
        pairs[1],
        w_in,
        specs=[whole(x) for x in pairs] + [of_expert(w_in)],
    )
    mine_sum, beside_sum = call(
        functools.partial(combine_body, cap),
        [bf(token_count, width)] * 2,
        macs // 4,
        LIMITS[5],
        scal,
        *backs,
        *[across(x, j) for j, x in enumerate(sent)],
    )
    input_grad = (mine_sum.astype(F32) + along_z(beside_sum, 1).astype(F32)).astype(BF)
    return (input_grad, grad_in, grad_down)


LIMITS = (24, 28, 28, 24, 24, 16)


def solution(mesh):
    in_specs = (
        P(("dp", "expert"), None),
        P(("dp", "expert"), None),
        P(("dp", "expert"), None),
        P(("dp", "expert"), None),
        P(("dp", "expert"), None),
        P("expert", None, None),
        P("expert", None, None),
    )
    out_specs = (P(("dp", "expert"), None), P("expert", "dp", None), P("expert", "dp", None))
    return jax.shard_map(
        per_device, mesh=mesh, in_specs=in_specs, out_specs=out_specs, check_vma=False
    )
```

```python
import functools

import jax
import jax.numpy as jnp
from jax import lax
from jax.experimental import pallas as pl
from jax.experimental.pallas import tpu as pltpu
from jax.sharding import PartitionSpec as P

TOP = 2
BF = jnp.bfloat16
F32 = jnp.float32
IN_PARTS = 1


def dot(a, b):
    return jnp.dot(a, b, preferred_element_type=F32)


def dot_nt(a, b):
    return lax.dot_general(a, b, (((1,), (1,)), ((), ())), preferred_element_type=F32)


def bf(*shape):
    return jax.ShapeDtypeStruct(shape, BF)


def whole(array):
    return pl.BlockSpec(array.shape, lambda step, scal: (0,) * len(array.shape))


def of_expert(weights, columns=None, index=0):
    shape = (1, weights.shape[1], columns or weights.shape[2])
    return pl.BlockSpec(shape, lambda step, scal: (scal[0], 0, index))


def call(body, out_shape, flops, limit, scal, *args, specs=None):
    return pl.pallas_call(
        body,
        out_shape=out_shape,
        grid_spec=pltpu.PrefetchScalarGridSpec(
            num_scalar_prefetch=1,
            grid=(1,),
            in_specs=specs or [whole(x) for x in args],
            out_specs=[whole(x) for x in out_shape],
        ),
        compiler_params=pltpu.CompilerParams(vmem_limit_bytes=limit << 20),
        cost_estimate=pl.CostEstimate(flops=flops, bytes_accessed=flops // 1000, transcendentals=0),
    )(scal, *args)


def stack_rows(refs, column, columns):
    return jnp.concatenate([ref[:, pl.ds(column, columns)] for ref in refs], axis=0)


def after(value, *others):
    return lax.optimization_barrier((value, *others))[0]


ROUTE_ROWS = 16


def route_rows(route_logits, expert_ids, slot_pos, width):
    share = jax.nn.sigmoid(route_logits[:, 0] - route_logits[:, 1])
    high = lax.reduce_precision(share, 8, 7)
    middle = lax.reduce_precision(share - high, 8, 7)
    low = share - high - middle
    places = jnp.concatenate(
        [x.astype(BF) for x in (expert_ids[:, 0], expert_ids[:, 1], slot_pos[:, 0], slot_pos[:, 1])]
    )
    shares = jnp.concatenate([x.astype(BF) for x in (high, middle, low)])
    rows = [jnp.pad(x, (0, width - x.shape[0])) for x in (places, shares)]
    return jnp.pad(jnp.stack(rows), ((0, ROUTE_ROWS - 2), (0, 0)))


def slots_body(cap, n, scal, block, *refs):
    outs, back = refs[:-1], refs[-1]
    tokens = back.shape[0]
    route = block[0:2, :].astype(F32)
    row = lambda r, k: route[r : r + 1, k * tokens : (k + 1) * tokens]
    slot = lax.broadcasted_iota(jnp.int32, (cap, tokens), 0)
    slot = jnp.concatenate([slot + scal[2 + j] for j in range(n)], axis=0).astype(F32)
    first = slot == row(0, 0) * cap + row(0, 2)
    second = slot == row(0, 1) * cap + row(0, 3)
    share = row(1, 0) + row(1, 1) + row(1, 2)
    hit = jnp.where(jnp.logical_or(first, second), 1.0, 0.0)
    factor = jnp.where(first, share, 0.0) + jnp.where(second, 1.0 - share, 0.0)
    factor = jnp.sum(factor, axis=1, keepdims=True)
    back[...] = jnp.transpose(hit).astype(BF)
    hit = hit.astype(BF)
    rows = dot(hit, block[pl.ds(ROUTE_ROWS, tokens), :]).astype(BF)
    scaled = (dot(hit, block[pl.ds(ROUTE_ROWS + tokens, tokens), :]) * factor).astype(BF)
    rows = jnp.concatenate([rows, scaled], axis=1)
    column = 0
    for k in range(0, len(outs), n):
        columns = outs[k].shape[1]
        for j in range(n):
            outs[k + j][...] = rows[j * cap : (j + 1) * cap, column : column + columns]
        column += columns


def forward_body(tile, scal, *refs):
    *arrived, w_in, rows_t, hidden_t, scale_gate, scale_up = refs
    ff = w_in.shape[2] // 2
    rows = stack_rows(arrived, 0, w_in.shape[1])
    rows_t[...] = jnp.transpose(rows)
    for f in range(0, ff, tile):
        gate = dot(rows, w_in[0, :, pl.ds(f, tile)])
        upper = dot(rows, w_in[0, :, pl.ds(ff + f, tile)])
        sg = jax.nn.sigmoid(gate)
        activated = gate * sg
        hidden_t[pl.ds(f, tile), :] = jnp.transpose((activated * upper).astype(BF))
        scale_gate[:, pl.ds(f, tile)] = (upper * sg * (1.0 + gate * (1.0 - sg))).astype(BF)
        scale_up[:, pl.ds(f, tile)] = activated.astype(BF)


def shard_rows(sources, scal, nz, part):
    taken = []
    for offset in (1 - scal[1], scal[1]):
        for shard in range(nz):
            start = pl.multiple_of((2 * shard + offset) * part, 16)
            taken.append(jnp.concatenate([x[pl.ds(start, part), :] for x in sources], axis=1))
    return jnp.concatenate(taken, axis=0)


def down_body(n, nz, scal, *refs):
    arrived, (w_down, hidden_a, hidden_b, *scales), outs = (
        refs[: 2 * n],
        refs[2 * n : 2 * n + 7],
        refs[2 * n + 7 :],
    )
    give, keep, *pairs = outs
    part, width = give.shape[1:]
    slots = [stack_rows(arrived[:n], width, width), stack_rows(arrived[n:], 0, width)]
    left = shard_rows((hidden_a, hidden_b), scal, nz, part)
    result = dot(left, jnp.concatenate(slots, axis=0)).astype(BF)
    for k in range(nz):
        give[k] = result[k * part : (k + 1) * part]
        keep[k] = result[(nz + k) * part : (nz + k + 1) * part]
    for g in range(2):
        grad_hidden = dot_nt(slots[g], w_down[0])
        scale_gate, scale_up = scales[2 * g : 2 * g + 2]
        ff = scale_gate.shape[1]
        pairs[g][:, pl.ds(0, ff)] = (grad_hidden * scale_gate[...].astype(F32)).astype(BF)
        pairs[g][:, pl.ds(ff, ff)] = (grad_hidden * scale_up[...].astype(F32)).astype(BF)


def input_weight_body(first, nz, scal, rows_a, rows_b, pair_a, pair_b, give, keep):
    part, columns = give.shape[1:]
    pair = jnp.concatenate(
        [pair_a[:, pl.ds(first, columns)], pair_b[:, pl.ds(first, columns)]], axis=0
    )
    result = dot(shard_rows((rows_a, rows_b), scal, nz, part), pair).astype(BF)
    for k in range(nz):
        give[k] = result[k * part : (k + 1) * part]
        keep[k] = result[(nz + k) * part : (nz + k + 1) * part]


def in_blocks(rows, width, columns):
    blocks = [(c, width, 0, rows, c // width * rows, 0) for c in range(0, columns - width + 1, width)]
    rest = columns % width
    first = columns - rest
    count = rest * rows // width
    for k in range(width // rest if rest else 0):
        blocks.append((first, rest, k * count, count, first // width * rows, k * rest))
    return blocks


def pack_body(nz, scal, keep_down, other_down, *refs):
    ins, out = refs[:-1], refs[-1]
    width = keep_down.shape[2]
    top = keep_down.shape[1]
    rows = ins[0].shape[1]
    for k in range(nz):
        out[k, pl.ds(0, top), :] = keep_down[k] + other_down[k]
        total = jnp.concatenate([x[k] + y[k] for x, y in zip(ins[::2], ins[1::2])], axis=1)
        for c, columns, r, count, place, column in in_blocks(rows, width, total.shape[1]):
            out[k, pl.ds(top + place, count), pl.ds(column, columns)] = total[
                r : r + count, c : c + columns
            ]


def unpack_body(sets, scal, terms, grad_in, grad_down):
    top, width = grad_down.shape[1:]
    rows, columns = grad_in.shape[1:]
    for e, members in enumerate(sets):
        total = functools.reduce(jnp.add, [terms[k].astype(F32) for k in members])
        grad_down[e] = total[:top]
        for c, some, r, count, place, column in in_blocks(rows, width, columns):
            grad_in[e, pl.ds(r, count), pl.ds(c, some)] = total[
                top + place : top + place + count, column : column + some
            ]


def returned_body(cap, scal, pair_a, pair_b, w_in, *outs):
    for g, pair in enumerate((pair_a, pair_b)):
        returned = dot_nt(pair[...], w_in[0]).astype(BF)
        for j, out in enumerate(outs):
            out[pl.ds(g * cap, cap), :] = returned[j * cap : (j + 1) * cap]


def combine_body(cap, scal, back_a, back_b, *refs):
    arrived, outs = refs[:-2], refs[-2:]
    for g, (back, out) in enumerate(zip((back_a, back_b), outs)):
        rows = jnp.concatenate([x[pl.ds(g * cap, cap), :] for x in arrived], axis=0)
        out[...] = dot(back[...], rows).astype(BF)


def per_device(tokens, cotangent, route_logits, expert_ids, slot_pos, w_in, w_down):
    token_count, width = tokens.shape
    experts, ff = w_down.shape[:2]
    n = lax.axis_size("expert")
    ndp = lax.axis_size("dp")
    nz = ndp // 2
    cap = 2 * TOP * token_count // (experts * n)
    slots = n * cap
    column, place = lax.axis_index("expert"), lax.axis_index("dp")
    z, core = place // 2, place % 2
    expert_of = lambda k: (k ^ (k >> 1)) & 1
    mine = expert_of(z)
    scal = [mine, core]
    scal += [((column ^ j) * experts + mine) * cap for j in range(n)]
    scal += [z ^ k for k in range(nz)]
    scal = jnp.stack(scal).astype(jnp.int32)
    swap_core = lambda x: lax.ppermute(x, "dp", [(i, i ^ 1) for i in range(ndp)])
    along_z = lambda x, k: lax.ppermute(x, "dp", [(i, i ^ (2 * k)) for i in range(ndp)]) if k else x
    across = lambda x, j: lax.ppermute(x, "expert", [(i, i ^ j) for i in range(n)]) if j else x
    same_core = [list(range(c, ndp, 2)) for c in range(2)]
    macs = 2 * slots * width * ff

    block = jnp.concatenate(
        [route_rows(route_logits, expert_ids, slot_pos, width), tokens, cotangent], axis=0
    )
    messages = ([2 * width], [width, width])
    arrived, backs = [], []
    for parts, block in zip(messages, (block, along_z(block, 1))):
        *sent, back = call(
            functools.partial(slots_body, cap, n),
            [bf(cap, c) for c in parts for _ in range(n)] + [bf(token_count, slots)],
            macs // 4,
            LIMITS[0],
            scal,
            block,
        )
        arrived.append([across(x, k % n) for k, x in enumerate(sent)])
        backs.append(back)

    forwards = []
    for g in range(2):
        pieces = arrived[g][:n]
        forwards.append(
            call(
                functools.partial(forward_body, 256),
                [bf(width, slots), bf(ff, slots), bf(slots, ff), bf(slots, ff)],
                2 * macs,
                LIMITS[1],
                scal,
                *pieces,
                w_in,
                specs=[whole(x) for x in pieces] + [of_expert(w_in)],
            )
        )
    (rows_a, hidden_a, *scales_a), (rows_b, hidden_b, *scales_b) = forwards

    args = arrived[0] + arrived[1][n:] + [w_down, hidden_a, hidden_b] + scales_a + scales_b
    specs = [whole(x) for x in args]
    specs[2 * n] = of_expert(w_down)
    give, keep, *pairs = call(
        functools.partial(down_body, n, nz),
        [bf(nz, ff // ndp, width)] * 2 + [bf(slots, 2 * ff)] * 2,
        4 * macs,
        LIMITS[2],
        scal,
        *args,
        specs=specs,
    )
    terms = [keep, swap_core(give)]

    columns = 2 * ff // IN_PARTS
    for k in range(IN_PARTS):
        give, keep = call(
            functools.partial(input_weight_body, k * columns, nz),
            [bf(nz, width // ndp, columns)] * 2,
            4 * macs // IN_PARTS,
            LIMITS[3],
            scal,
            rows_a,
            rows_b,
            *pairs,
        )
        terms += [keep, swap_core(give)]
    sent = call(
        functools.partial(returned_body, cap),
        [bf(2 * cap, width)] * n,
        4 * macs,
        LIMITS[4],
        scal,
        pairs[0],
        pairs[1],
        w_in,
        specs=[whole(x) for x in pairs] + [of_expert(w_in)],
    )
    terms[-1] = after(terms[-1], *sent)
    rows = ff // ndp + width // ndp * 2 * ff // width
    (total,) = call(
        functools.partial(pack_body, nz), [bf(nz, rows, width)], 1, LIMITS[6], scal, *terms
    )
    total = lax.all_to_all(total, "dp", 0, 0, tiled=True, axis_index_groups=same_core)
    sets = [[k for k in range(nz) if expert_of(k) == e] for e in range(experts)]
    grad_in, grad_down = call(
        functools.partial(unpack_body, sets),
        [
            jax.ShapeDtypeStruct((experts, width // ndp, 2 * ff), F32),
            jax.ShapeDtypeStruct((experts, ff // ndp, width), F32),
        ],
        1,
        LIMITS[6],
        scal,
        total,
    )
    mine_sum, beside_sum = call(
        functools.partial(combine_body, cap),
        [bf(token_count, width)] * 2,
        macs // 4,
        LIMITS[5],
        scal,
        *backs,
        *[across(x, j) for j, x in enumerate(sent)],
    )
    input_grad = (mine_sum.astype(F32) + along_z(beside_sum, 1).astype(F32)).astype(BF)
    return (input_grad, grad_in, grad_down)


LIMITS = (16, 20, 20, 20, 20, 12, 20)


def solution(mesh):
    in_specs = (
        P(("dp", "expert"), None),
        P(("dp", "expert"), None),
        P(("dp", "expert"), None),
        P(("dp", "expert"), None),
        P(("dp", "expert"), None),
        P("expert", None, None),
        P("expert", None, None),
    )
    out_specs = (P(("dp", "expert"), None), P("expert", "dp", None), P("expert", "dp", None))
    return jax.shard_map(
        per_device, mesh=mesh, in_specs=in_specs, out_specs=out_specs, check_vma=False
    )
```

```python
import functools

import jax
import jax.numpy as jnp
from jax import lax
from jax.experimental import pallas as pl
from jax.experimental.pallas import tpu as pltpu
from jax.sharding import PartitionSpec as P

TOP = 2
BF = jnp.bfloat16
F32 = jnp.float32
IN_PARTS = 1


def dot(a, b):
    return jnp.dot(a, b, preferred_element_type=F32)


def dot_nt(a, b):
    return lax.dot_general(a, b, (((1,), (1,)), ((), ())), preferred_element_type=F32)


def bf(*shape):
    return jax.ShapeDtypeStruct(shape, BF)


def whole(array):
    return pl.BlockSpec(array.shape, lambda step, scal: (0,) * len(array.shape))


def of_expert(weights, columns=None, index=0):
    shape = (1, weights.shape[1], columns or weights.shape[2])
    return pl.BlockSpec(shape, lambda step, scal: (scal[0], 0, index))


def call(body, out_shape, flops, limit, scal, *args, specs=None):
    return pl.pallas_call(
        body,
        out_shape=out_shape,
        grid_spec=pltpu.PrefetchScalarGridSpec(
            num_scalar_prefetch=1,
            grid=(1,),
            in_specs=specs or [whole(x) for x in args],
            out_specs=[whole(x) for x in out_shape],
        ),
        compiler_params=pltpu.CompilerParams(vmem_limit_bytes=limit << 20),
        cost_estimate=pl.CostEstimate(flops=flops, bytes_accessed=flops // 1000, transcendentals=0),
    )(scal, *args)


def stack_rows(refs, column, columns):
    return jnp.concatenate([ref[:, pl.ds(column, columns)] for ref in refs], axis=0)


def in_hbm(value):
    return pltpu.with_memory_space_constraint(value, pltpu.HBM)


def after(value, *others):
    return lax.optimization_barrier((value, *others))[0]


ROUTE_ROWS = 16


def fill_slots(cap, n, scal, route, tokens, cotangent, outs, back):
    chosen, places, share = route
    slot = lax.broadcasted_iota(jnp.int32, (cap, back.shape[0]), 0)
    slot = jnp.concatenate([slot + scal[2 + j] for j in range(n)], axis=0).astype(F32)
    first = slot == chosen[0] * cap + places[0]
    second = slot == chosen[1] * cap + places[1]
    hit = jnp.where(jnp.logical_or(first, second), 1.0, 0.0)
    factor = jnp.where(first, share, 0.0) + jnp.where(second, 1.0 - share, 0.0)
    factor = jnp.sum(factor, axis=1, keepdims=True)
    back[...] = jnp.transpose(hit).astype(BF)
    hit = hit.astype(BF)
    rows = dot(hit, tokens).astype(BF)
    scaled = (dot(hit, cotangent) * factor).astype(BF)
    rows = jnp.concatenate([rows, scaled], axis=1)
    column = 0
    for k in range(0, len(outs), n):
        columns = outs[k].shape[1]
        for j in range(n):
            outs[k + j][...] = rows[j * cap : (j + 1) * cap, column : column + columns]
        column += columns


def own_slots_body(cap, n, scal, logits, experts, places, tokens, cotangent, *refs):
    outs, back, block = refs[:-2], refs[-2], refs[-1]
    count, width = tokens.shape
    share = jax.nn.sigmoid(logits[0:1, :] - logits[1:2, :])
    high = share.astype(BF)
    middle = (share - high.astype(F32)).astype(BF)
    low = (share - high.astype(F32) - middle.astype(F32)).astype(BF)
    chosen = experts[...].astype(F32)
    slots = places[...].astype(F32)
    rows = [x.astype(BF).astype(F32) for x in (chosen[0:1], chosen[1:2], slots[0:1], slots[1:2])]
    shares = [x.astype(F32) for x in (high, middle, low)]
    shares.append(jnp.zeros_like(share))
    pad = [jnp.zeros((1, width - 4 * count), F32)] if width > 4 * count else []
    head = [jnp.concatenate(x + pad, axis=1) for x in (rows, shares)]
    head.append(jnp.zeros((ROUTE_ROWS - 2, width), F32))
    block[pl.ds(0, ROUTE_ROWS), :] = jnp.concatenate(head, axis=0).astype(BF)
    block[pl.ds(ROUTE_ROWS, count), :] = tokens[...]
    block[pl.ds(ROUTE_ROWS + count, count), :] = cotangent[...]
    route = ((chosen[0:1], chosen[1:2]), (slots[0:1], slots[1:2]), share)
    fill_slots(cap, n, scal, route, tokens[...], cotangent[...], outs, back)


def beside_slots_body(cap, n, scal, block, *refs):
    outs, back = refs[:-1], refs[-1]
    count = back.shape[0]
    head = block[0:2, :].astype(F32)
    row = lambda r, k: head[r : r + 1, k * count : (k + 1) * count]
    share = row(1, 0) + row(1, 1) + row(1, 2)
    route = ((row(0, 0), row(0, 1)), (row(0, 2), row(0, 3)), share)
    tokens = block[pl.ds(ROUTE_ROWS, count), :]
    fill_slots(cap, n, scal, route, tokens, block[pl.ds(ROUTE_ROWS + count, count), :], outs, back)


def forward_body(tile, scal, *refs):
    *arrived, w_in, rows_t, hidden_t, scale_gate, scale_up = refs
    ff = w_in.shape[2] // 2
    rows = stack_rows(arrived, 0, w_in.shape[1])
    rows_t[...] = jnp.transpose(rows)
    for f in range(0, ff, tile):
        gate = dot(rows, w_in[0, :, pl.ds(f, tile)])
        upper = dot(rows, w_in[0, :, pl.ds(ff + f, tile)])
        sg = jax.nn.sigmoid(gate)
        activated = gate * sg
        hidden_t[pl.ds(f, tile), :] = jnp.transpose((activated * upper).astype(BF))
        scale_gate[:, pl.ds(f, tile)] = (upper * sg * (1.0 + gate * (1.0 - sg))).astype(BF)
        scale_up[:, pl.ds(f, tile)] = activated.astype(BF)


def shard_rows(sources, scal, nz, part):
    taken = []
    for offset in (1 - scal[1], scal[1]):
        for shard in range(nz):
            start = pl.multiple_of((2 * shard + offset) * part, 16)
            taken.append(jnp.concatenate([x[pl.ds(start, part), :] for x in sources], axis=1))
    return jnp.concatenate(taken, axis=0)


def pair_body(column, scal, *refs):
    *arrived, w_down, scale_gate, scale_up, pair = refs
    grad_hidden = dot_nt(stack_rows(arrived, column, w_down.shape[2]), w_down[0])
    ff = scale_gate.shape[1]
    pair[:, pl.ds(0, ff)] = (grad_hidden * scale_gate[...].astype(F32)).astype(BF)
    pair[:, pl.ds(ff, ff)] = (grad_hidden * scale_up[...].astype(F32)).astype(BF)


def down_body(n, nz, scal, *refs):
    arrived, (hidden_a, hidden_b, give, keep) = refs[: 2 * n], refs[2 * n :]
    part, width = give.shape[1:]
    slots = [stack_rows(arrived[:n], width, width), stack_rows(arrived[n:], 0, width)]
    left = shard_rows((hidden_a, hidden_b), scal, nz, part)
    result = dot(left, jnp.concatenate(slots, axis=0)).astype(BF)
    for k in range(nz):
        give[k] = result[k * part : (k + 1) * part]
        keep[k] = result[(nz + k) * part : (nz + k + 1) * part]


def input_weight_body(first, nz, scal, rows_a, rows_b, pair_a, pair_b, give, keep):
    part, columns = give.shape[1:]
    pair = jnp.concatenate(
        [pair_a[:, pl.ds(first, columns)], pair_b[:, pl.ds(first, columns)]], axis=0
    )
    result = dot(shard_rows((rows_a, rows_b), scal, nz, part), pair).astype(BF)
    for k in range(nz):
        give[k] = result[k * part : (k + 1) * part]
        keep[k] = result[(nz + k) * part : (nz + k + 1) * part]


def in_blocks(rows, width, columns):
    blocks = [(c, width, 0, rows, c // width * rows, 0) for c in range(0, columns - width + 1, width)]
    rest = columns % width
    first = columns - rest
    count = rest * rows // width
    for k in range(width // rest if rest else 0):
        blocks.append((first, rest, k * count, count, first // width * rows, k * rest))
    return blocks


def pack_body(nz, scal, keep_down, other_down, *refs):
    ins, out = refs[:-1], refs[-1]
    width = keep_down.shape[2]
    top = keep_down.shape[1]
    rows = ins[0].shape[1]
    for k in range(nz):
        out[k, pl.ds(0, top), :] = keep_down[k] + other_down[k]
        total = jnp.concatenate([x[k] + y[k] for x, y in zip(ins[::2], ins[1::2])], axis=1)
        for c, columns, r, count, place, column in in_blocks(rows, width, total.shape[1]):
            out[k, pl.ds(top + place, count), pl.ds(column, columns)] = total[
                r : r + count, c : c + columns
            ]


def unpack_body(sets, scal, terms, grad_in, grad_down):
    top, width = grad_down.shape[1:]
    rows, columns = grad_in.shape[1:]
    for e, members in enumerate(sets):
        total = functools.reduce(jnp.add, [terms[k].astype(F32) for k in members])
        grad_down[e] = total[:top]
        for c, some, r, count, place, column in in_blocks(rows, width, columns):
            grad_in[e, pl.ds(r, count), pl.ds(c, some)] = total[
                top + place : top + place + count, column : column + some
            ]


def returned_body(cap, scal, pair, w_in, *outs):
    returned = dot_nt(pair[...], w_in[0]).astype(BF)
    for j, out in enumerate(outs):
        out[...] = returned[j * cap : (j + 1) * cap]


def combine_body(scal, back, *refs):
    *arrived, out = refs
    out[...] = dot(back[...], stack_rows(arrived, 0, out.shape[1])).astype(BF)


def per_device(tokens, cotangent, route_logits, expert_ids, slot_pos, w_in, w_down):
    token_count, width = tokens.shape
    experts, ff = w_down.shape[:2]
    n = lax.axis_size("expert")
    ndp = lax.axis_size("dp")
    nz = ndp // 2
    cap = 2 * TOP * token_count // (experts * n)
    slots = n * cap
    column, place = lax.axis_index("expert"), lax.axis_index("dp")
    z, core = place // 2, place % 2
    expert_of = lambda k: (k ^ (k >> 1)) & 1
    mine = expert_of(z)
    scal = [mine, core]
    scal += [((column ^ j) * experts + mine) * cap for j in range(n)]
    scal += [z ^ k for k in range(nz)]
    scal = jnp.stack(scal).astype(jnp.int32)
    swap_core = lambda x: lax.ppermute(x, "dp", [(i, i ^ 1) for i in range(ndp)])
    along_z = lambda x, k: lax.ppermute(x, "dp", [(i, i ^ (2 * k)) for i in range(ndp)]) if k else x
    across = lambda x, j: lax.ppermute(x, "expert", [(i, i ^ j) for i in range(n)]) if j else x
    same_core = [list(range(c, ndp, 2)) for c in range(2)]
    macs = 2 * slots * width * ff

    count = token_count
    *sent, back, block = call(
        functools.partial(own_slots_body, cap, n),
        [bf(cap, 2 * width)] * n + [bf(count, slots), bf(ROUTE_ROWS + 2 * count, width)],
        macs // 4,
        LIMITS[0],
        scal,
        *[in_hbm(x) for x in (route_logits.T, expert_ids.T, slot_pos.T, tokens, cotangent)],
    )
    arrived = [[across(x, j) for j, x in enumerate(sent)]]
    *sent, back_beside = call(
        functools.partial(beside_slots_body, cap, n),
        [bf(cap, width)] * (2 * n) + [bf(count, slots)],
        macs // 4,
        LIMITS[0],
        scal,
        along_z(block, 1),
    )
    arrived.append([across(x, k % n) for k, x in enumerate(sent)])
    backs = [back, back_beside]

    forwards = []
    for g in range(2):
        pieces = arrived[g][:n]
        forwards.append(
            call(
                functools.partial(forward_body, 256),
                [bf(width, slots), bf(ff, slots), bf(slots, ff), bf(slots, ff)],
                2 * macs,
                LIMITS[1],
                scal,
                *pieces,
                w_in,
                specs=[whole(x) for x in pieces] + [of_expert(w_in)],
            )
        )
    (rows_a, hidden_a, *scales_a), (rows_b, hidden_b, *scales_b) = forwards

    pairs = []
    for g, (column, scales) in enumerate(((width, scales_a), (0, scales_b))):
        pieces = arrived[g][-n:]
        args = pieces + [w_down] + scales
        pairs += call(
            functools.partial(pair_body, column),
            [bf(slots, 2 * ff)],
            macs,
            LIMITS[2],
            scal,
            *args,
            specs=[whole(x) for x in pieces] + [of_expert(w_down)] + [whole(x) for x in scales],
        )

    columns = 2 * ff // IN_PARTS
    terms = []
    for k in range(IN_PARTS):
        give, keep = call(
            functools.partial(input_weight_body, k * columns, nz),
            [bf(nz, width // ndp, columns)] * 2,
            4 * macs // IN_PARTS,
            LIMITS[3],
            scal,
            rows_a,
            rows_b,
            *pairs,
        )
        terms += [keep, swap_core(give)]
    give, keep = call(
        functools.partial(down_body, n, nz),
        [bf(nz, ff // ndp, width)] * 2,
        2 * macs,
        LIMITS[2],
        scal,
        *arrived[0],
        *arrived[1][n:],
        hidden_a,
        hidden_b,
    )
    terms = [keep, swap_core(give)] + terms
    returned = [
        call(
            functools.partial(returned_body, cap),
            [bf(cap, width)] * n,
            2 * macs,
            LIMITS[4],
            scal,
            pair,
            w_in,
            specs=[whole(pair), of_expert(w_in)],
        )
        for pair in pairs
    ]
    rows = ff // ndp + width // ndp * 2 * ff // width
    (total,) = call(
        functools.partial(pack_body, nz), [bf(nz, rows, width)], 1, LIMITS[6], scal, *terms
    )
    total = lax.all_to_all(total, "dp", 0, 0, tiled=True, axis_index_groups=same_core)
    sets = [[k for k in range(nz) if expert_of(k) == e] for e in range(experts)]
    grad_in, grad_down = call(
        functools.partial(unpack_body, sets),
        [
            jax.ShapeDtypeStruct((experts, width // ndp, 2 * ff), F32),
            jax.ShapeDtypeStruct((experts, ff // ndp, width), F32),
        ],
        1,
        LIMITS[6],
        scal,
        total,
    )
    sums = []
    for sent, back in zip(returned, backs):
        arrived = [across(x, j) for j, x in enumerate(sent)]
        sums += call(combine_body, [bf(count, width)], macs // 8, LIMITS[5], scal, back, *arrived)
    mine_sum, beside_sum = sums
    input_grad = (mine_sum.astype(F32) + along_z(beside_sum, 1).astype(F32)).astype(BF)
    return (input_grad, grad_in, grad_down)


LIMITS = (16, 20, 20, 20, 20, 12, 20)


def solution(mesh):
    in_specs = (
        P(("dp", "expert"), None),
        P(("dp", "expert"), None),
        P(("dp", "expert"), None),
        P(("dp", "expert"), None),
        P(("dp", "expert"), None),
        P("expert", None, None),
        P("expert", None, None),
    )
    out_specs = (P(("dp", "expert"), None), P("expert", "dp", None), P("expert", "dp", None))
    return jax.shard_map(
        per_device, mesh=mesh, in_specs=in_specs, out_specs=out_specs, check_vma=False
    )
```

```python
import functools

import jax
import jax.numpy as jnp
from jax import lax
from jax.experimental import pallas as pl
from jax.experimental.pallas import tpu as pltpu
from jax.sharding import PartitionSpec as P

TOP = 2
BF = jnp.bfloat16
F32 = jnp.float32


def dot(a, b):
    return jnp.dot(a, b, preferred_element_type=F32)


def dot_nt(a, b):
    return lax.dot_general(a, b, (((1,), (1,)), ((), ())), preferred_element_type=F32)


def bf(*shape):
    return jax.ShapeDtypeStruct(shape, BF)


def whole(array):
    return pl.BlockSpec(array.shape, lambda step, scal: (0,) * len(array.shape))


def of_expert(weights, columns=None, index=0):
    shape = (1, weights.shape[1], columns or weights.shape[2])
    return pl.BlockSpec(shape, lambda step, scal: (scal[0], 0, index))


def call(body, out_shape, flops, limit, scal, *args, specs=None, out_specs=None, steps=1):
    params = dict(
        out_shape=out_shape,
        compiler_params=pltpu.CompilerParams(vmem_limit_bytes=limit << 20),
        cost_estimate=pl.CostEstimate(flops=flops, bytes_accessed=flops // 1000, transcendentals=0),
    )
    if specs is None:
        vmem = pl.BlockSpec(memory_space=pltpu.VMEM)
        params.update(
            in_specs=[pl.BlockSpec(memory_space=pltpu.SMEM)] + [vmem] * len(args),
            out_specs=[vmem] * len(out_shape),
        )
    else:
        params["grid_spec"] = pltpu.PrefetchScalarGridSpec(
            num_scalar_prefetch=1,
            grid=(steps,),
            in_specs=specs,
            out_specs=out_specs or [whole(x) for x in out_shape],
        )
    return pl.pallas_call(body, **params)(scal, *args)


def stack_rows(refs, column, columns):
    return jnp.concatenate([ref[:, pl.ds(column, columns)] for ref in refs], axis=0)


def in_hbm(value):
    return pltpu.with_memory_space_constraint(value, pltpu.HBM)


def after(value, *others):
    return lax.optimization_barrier((value, *others))[0]


ROUTE_ROWS = 16


def slot_hits(cap, n, scal, route, count):
    chosen, places, _ = route
    slot = lax.broadcasted_iota(jnp.int32, (cap, count), 0)
    slot = jnp.concatenate([slot + scal[2 + j] for j in range(n)], axis=0).astype(F32)
    return slot == chosen[0] * cap + places[0], slot == chosen[1] * cap + places[1]


def token_rows(hits, tokens, back):
    hit = jnp.where(jnp.logical_or(*hits), 1.0, 0.0)
    back[...] = jnp.transpose(hit).astype(BF)
    return dot(hit.astype(BF), tokens).astype(BF)


def cotangent_rows(hits, share, cotangent):
    hit = jnp.where(jnp.logical_or(*hits), 1.0, 0.0).astype(BF)
    factor = jnp.where(hits[0], share, 0.0) + jnp.where(hits[1], 1.0 - share, 0.0)
    return (dot(hit, cotangent) * jnp.sum(factor, axis=1, keepdims=True)).astype(BF)


def own_slots_body(cap, n, scal, logits, experts, places, tokens, cotangent, *refs):
    outs, back, block = refs[:-2], refs[-2], refs[-1]
    count, width = tokens.shape
    share = jax.nn.sigmoid(logits[0:1, :] - logits[1:2, :])
    high = share.astype(BF)
    middle = (share - high.astype(F32)).astype(BF)
    low = (share - high.astype(F32) - middle.astype(F32)).astype(BF)
    chosen = experts[...].astype(F32)
    slots = places[...].astype(F32)
    rows = [chosen[0:1], chosen[1:2], slots[0:1], slots[1:2]]
    shares = [x.astype(F32) for x in (high, middle, low)]
    shares.append(jnp.zeros_like(share))
    pad = [jnp.zeros((1, width - 4 * count), F32)] if width > 4 * count else []
    head = [jnp.concatenate(x + pad, axis=1) for x in (rows, shares)]
    head.append(jnp.zeros((ROUTE_ROWS - 2, width), F32))
    block[pl.ds(0, ROUTE_ROWS), :] = jnp.concatenate(head, axis=0).astype(BF)
    block[pl.ds(ROUTE_ROWS, count), :] = tokens[...]
    route = ((chosen[0:1], chosen[1:2]), (slots[0:1], slots[1:2]), share)
    hits = slot_hits(cap, n, scal, route, count)
    rows = token_rows(hits, tokens[...], back)
    scaled = cotangent_rows(hits, share, cotangent[...])
    for j, out in enumerate(outs):
        out[:, pl.ds(0, width)] = rows[j * cap : (j + 1) * cap]
        out[:, pl.ds(width, width)] = scaled[j * cap : (j + 1) * cap]


def read_route(block, count):
    head = block[0:2, :].astype(F32)
    row = lambda r, k: head[r : r + 1, k * count : (k + 1) * count]
    share = row(1, 0) + row(1, 1) + row(1, 2)
    return (row(0, 0), row(0, 1)), (row(0, 2), row(0, 3)), share


def beside_tokens_body(cap, n, scal, block, *refs):
    outs, back = refs[:-1], refs[-1]
    count = back.shape[0]
    hits = slot_hits(cap, n, scal, read_route(block, count), count)
    rows = token_rows(hits, block[pl.ds(ROUTE_ROWS, count), :], back)
    for j, out in enumerate(outs):
        out[...] = rows[j * cap : (j + 1) * cap]


def beside_cotangents_body(cap, n, scal, block, cotangent, *outs):
    count = cotangent.shape[0]
    route = read_route(block, count)
    rows = cotangent_rows(slot_hits(cap, n, scal, route, count), route[2], cotangent[...])
    for j, out in enumerate(outs):
        out[...] = rows[j * cap : (j + 1) * cap]


def forward_body(tile, scal, *refs):
    *arrived, w_in, rows_t, hidden_t, scale_gate, scale_up = refs
    ff = w_in.shape[2] // 2
    rows = stack_rows(arrived, 0, w_in.shape[1])
    rows_t[...] = jnp.transpose(rows)
    for f in range(0, ff, tile):
        gate = dot(rows, w_in[0, :, pl.ds(f, tile)])
        upper = dot(rows, w_in[0, :, pl.ds(ff + f, tile)])
        sg = jax.nn.sigmoid(gate)
        activated = gate * sg
        hidden_t[pl.ds(f, tile), :] = jnp.transpose((activated * upper).astype(BF))
        scale_gate[:, pl.ds(f, tile)] = (upper * sg * (1.0 + gate * (1.0 - sg))).astype(BF)
        scale_up[:, pl.ds(f, tile)] = activated.astype(BF)


def shard_rows(sources, scal, nz, part):
    taken = []
    for offset in (1 - scal[1], scal[1]):
        for shard in range(nz):
            start = pl.multiple_of((2 * shard + offset) * part, 16)
            taken.append(jnp.concatenate([x[pl.ds(start, part), :] for x in sources], axis=1))
    return jnp.concatenate(taken, axis=0)


def pair_body(column, scal, *refs):
    *arrived, w_down, scale_gate, scale_up, pair = refs
    grad_hidden = dot_nt(stack_rows(arrived, column, w_down.shape[2]), w_down[0])
    ff = scale_gate.shape[1]
    pair[:, pl.ds(0, ff)] = (grad_hidden * scale_gate[...].astype(F32)).astype(BF)
    pair[:, pl.ds(ff, ff)] = (grad_hidden * scale_up[...].astype(F32)).astype(BF)


def put_shards(result, nz, part, before, give, keep):
    for k in range(nz):
        for out, earlier, first in ((give, before[:1], k), (keep, before[1:], nz + k)):
            total = result[first * part : (first + 1) * part]
            for x in earlier:
                total = total + x[k].astype(F32)
            out[k] = total.astype(BF)


def down_body(n, nz, column, scal, *refs):
    arrived, hidden, before, (give, keep) = refs[:n], refs[n], refs[n + 1 : -2], refs[-2:]
    part, width = give.shape[1:]
    left = shard_rows((hidden,), scal, nz, part)
    put_shards(dot(left, stack_rows(arrived, column, width)), nz, part, before, give, keep)


def input_weight_body(nz, scal, rows, pair, *refs):
    before, (give, keep) = refs[:-2], refs[-2:]
    part = give.shape[1]
    left = shard_rows((rows,), scal, nz, part)
    put_shards(dot(left, pair[...]), nz, part, before, give, keep)


def in_blocks(rows, width, columns):
    blocks = [(c, width, 0, rows, c // width * rows, 0) for c in range(0, columns - width + 1, width)]
    rest = columns % width
    first = columns - rest
    count = rest * rows // width
    for k in range(width // rest if rest else 0):
        blocks.append((first, rest, k * count, count, first // width * rows, k * rest))
    return blocks


def pack_body(scal, keep_down, other_down, *refs):
    ins, out = refs[:-1], refs[-1]
    width = keep_down.shape[2]
    top = keep_down.shape[1]
    rows = ins[0].shape[1]
    out[0, pl.ds(0, top), :] = keep_down[0] + other_down[0]
    total = jnp.concatenate([x[0] + y[0] for x, y in zip(ins[::2], ins[1::2])], axis=1)
    for c, columns, r, count, place, column in in_blocks(rows, width, total.shape[1]):
        out[0, pl.ds(top + place, count), pl.ds(column, columns)] = total[
            r : r + count, c : c + columns
        ]


def unpack_body(scal, *refs):
    terms, (grad_in, grad_down) = refs[:-2], refs[-2:]
    top, width = grad_down.shape[1:]
    rows, columns = grad_in.shape[1:]
    total = functools.reduce(jnp.add, [x[0].astype(F32) for x in terms])
    grad_down[0] = total[:top]
    for c, some, r, count, place, column in in_blocks(rows, width, columns):
        grad_in[0, pl.ds(r, count), pl.ds(c, some)] = total[
            top + place : top + place + count, column : column + some
        ]


def returned_body(cap, scal, pair, w_in, *outs):
    returned = dot_nt(pair[...], w_in[0]).astype(BF)
    for j, out in enumerate(outs):
        out[...] = returned[j * cap : (j + 1) * cap]


def combine_body(scal, back, *refs):
    *arrived, out = refs
    out[...] = dot(back[...], stack_rows(arrived, 0, out.shape[1])).astype(BF)


def per_device(tokens, cotangent, route_logits, expert_ids, slot_pos, w_in, w_down):
    token_count, width = tokens.shape
    experts, ff = w_down.shape[:2]
    n = lax.axis_size("expert")
    ndp = lax.axis_size("dp")
    nz = ndp // 2
    cap = 2 * TOP * token_count // (experts * n)
    slots = n * cap
    column, place = lax.axis_index("expert"), lax.axis_index("dp")
    z, core = place // 2, place % 2
    expert_of = lambda k: (k ^ (k >> 1)) & 1
    mine = expert_of(z)
    scal = [mine, core]
    scal += [((column ^ j) * experts + mine) * cap for j in range(n)]
    scal += [z ^ k for k in range(nz)]
    scal = jnp.stack(scal).astype(jnp.int32)
    swap_core = lambda x: lax.ppermute(x, "dp", [(i, i ^ 1) for i in range(ndp)])
    along_z = lambda x, k: lax.ppermute(x, "dp", [(i, i ^ (2 * k)) for i in range(ndp)]) if k else x
    across = lambda x, j: lax.ppermute(x, "expert", [(i, i ^ j) for i in range(n)]) if j else x
    same_core = [list(range(c, ndp, 2)) for c in range(2)]
    macs = 2 * slots * width * ff

    count = token_count
    held = [in_hbm(x) for x in (route_logits.T, expert_ids.T, slot_pos.T, tokens, cotangent)]
    *sent, back, block = call(
        functools.partial(own_slots_body, cap, n),
        [bf(cap, 2 * width)] * n + [bf(count, slots), bf(ROUTE_ROWS + count, width)],
        macs // 4,
        LIMITS[0],
        scal,
        *held,
        specs=[whole(x) for x in held],
    )
    arrived = [[across(x, j) for j, x in enumerate(sent)]]
    block = along_z(block, 1)
    cotangent = along_z(cotangent, 1)
    *sent, back_beside = call(
        functools.partial(beside_tokens_body, cap, n),
        [bf(cap, width)] * n + [bf(count, slots)],
        macs // 8,
        LIMITS[0],
        scal,
        block,
    )
    scaled = call(
        functools.partial(beside_cotangents_body, cap, n),
        [bf(cap, width)] * n,
        macs // 8,
        LIMITS[0],
        scal,
        block,
        cotangent,
    )
    arrived.append([across(x, j) for x_all in (sent, scaled) for j, x in enumerate(x_all)])
    backs = [back, back_beside]

    forwards = []
    for g in range(2):
        pieces = arrived[g][:n]
        forwards.append(
            call(
                functools.partial(forward_body, 256),
                [bf(width, slots), bf(ff, slots), bf(slots, ff), bf(slots, ff)],
                2 * macs,
                LIMITS[1],
                scal,
                *pieces,
                w_in,
                specs=[whole(x) for x in pieces] + [of_expert(w_in)],
            )
        )
    (rows_a, hidden_a, *scales_a), (rows_b, hidden_b, *scales_b) = forwards

    pairs = []
    for g, (column, scales) in enumerate(((width, scales_a), (0, scales_b))):
        pieces = arrived[g][-n:]
        args = pieces + [w_down] + scales
        pairs += call(
            functools.partial(pair_body, column),
            [bf(slots, 2 * ff)],
            macs,
            LIMITS[2],
            scal,
            *args,
            specs=[whole(x) for x in pieces] + [of_expert(w_down)] + [whole(x) for x in scales],
        )

    ins, downs = [], []
    for rows, pair in zip((rows_a, rows_b), pairs):
        ins = call(
            functools.partial(input_weight_body, nz),
            [bf(nz, width // ndp, 2 * ff)] * 2,
            2 * macs,
            LIMITS[3],
            scal,
            rows,
            pair,
            *ins,
        )
    for g, (column, hidden) in enumerate(((width, hidden_a), (0, hidden_b))):
        downs = call(
            functools.partial(down_body, n, nz, column),
            [bf(nz, ff // ndp, width)] * 2,
            macs,
            LIMITS[2],
            scal,
            *arrived[g][-n:],
            hidden,
            *downs,
        )
    terms = [downs[1], swap_core(downs[0]), ins[1], swap_core(ins[0])]
    returned = [
        call(
            functools.partial(returned_body, cap),
            [bf(cap, width)] * n,
            2 * macs,
            LIMITS[4],
            scal,
            pair,
            w_in,
            specs=[whole(pair), of_expert(w_in)],
        )
        for pair in pairs
    ]
    rows = ff // ndp + width // ndp * 2 * ff // width
    by_z = lambda x: pl.BlockSpec((1,) + x.shape[1:], lambda k, scal: (k, 0, 0))
    packed = bf(nz, rows, width)
    (total,) = call(
        pack_body,
        [packed],
        1,
        LIMITS[6],
        scal,
        *terms,
        specs=[by_z(x) for x in terms],
        out_specs=[by_z(packed)],
        steps=nz,
    )
    total = lax.all_to_all(total, "dp", 0, 0, tiled=True, axis_index_groups=same_core)
    sets = [[k for k in range(nz) if expert_of(k) == e] for e in range(experts)]
    members = jnp.array(sets, jnp.int32).reshape(-1)
    many = len(sets[0])
    by_expert = lambda *shape: pl.BlockSpec((1,) + shape, lambda e, scal: (e, 0, 0))
    grad_in, grad_down = call(
        unpack_body,
        [
            jax.ShapeDtypeStruct((experts, width // ndp, 2 * ff), F32),
            jax.ShapeDtypeStruct((experts, ff // ndp, width), F32),
        ],
        1,
        LIMITS[6],
        members,
        *[total] * many,
        specs=[
            pl.BlockSpec((1,) + total.shape[1:], lambda e, scal, m=m: (scal[e * many + m], 0, 0))
            for m in range(many)
        ],
        out_specs=[by_expert(width // ndp, 2 * ff), by_expert(ff // ndp, width)],
        steps=experts,
    )
    sums = []
    for sent, back in zip(returned, backs):
        arrived = [across(x, j) for j, x in enumerate(sent)]
        sums += call(combine_body, [bf(count, width)], macs // 8, LIMITS[5], scal, back, *arrived)
    mine_sum, beside_sum = sums
    input_grad = (mine_sum.astype(F32) + along_z(beside_sum, 1).astype(F32)).astype(BF)
    return (input_grad, grad_in, grad_down)


LIMITS = (16, 20, 20, 20, 20, 12, 20)


def solution(mesh):
    in_specs = (
        P(("dp", "expert"), None),
        P(("dp", "expert"), None),
        P(("dp", "expert"), None),
        P(("dp", "expert"), None),
        P(("dp", "expert"), None),
        P("expert", None, None),
        P("expert", None, None),
    )
    out_specs = (P(("dp", "expert"), None), P("expert", "dp", None), P("expert", "dp", None))
    return jax.shard_map(
        per_device, mesh=mesh, in_specs=in_specs, out_specs=out_specs, check_vma=False
    )
```

```python
import functools

import jax
import jax.numpy as jnp
from jax import lax
from jax.experimental import pallas as pl
from jax.experimental.pallas import tpu as pltpu
from jax.sharding import PartitionSpec as P

TOP = 2
BF = jnp.bfloat16
F32 = jnp.float32


def dot(a, b):
    return jnp.dot(a, b, preferred_element_type=F32)


def dot_nt(a, b):
    return lax.dot_general(a, b, (((1,), (1,)), ((), ())), preferred_element_type=F32)


def bf(*shape):
    return jax.ShapeDtypeStruct(shape, BF)


def whole(array):
    return pl.BlockSpec(array.shape, lambda step, scal: (0,) * len(array.shape))


def of_expert(weights, columns=None, index=0):
    shape = (1, weights.shape[1], columns or weights.shape[2])
    return pl.BlockSpec(shape, lambda step, scal: (scal[0], 0, index))


def call(body, out_shape, flops, limit, scal, *args, specs=None, out_specs=None, steps=1):
    params = dict(
        out_shape=out_shape,
        compiler_params=pltpu.CompilerParams(vmem_limit_bytes=limit << 20),
        cost_estimate=pl.CostEstimate(flops=flops, bytes_accessed=flops // 1000, transcendentals=0),
    )
    if specs is None:
        vmem = pl.BlockSpec(memory_space=pltpu.VMEM)
        params.update(
            in_specs=[pl.BlockSpec(memory_space=pltpu.SMEM)] + [vmem] * len(args),
            out_specs=[vmem] * len(out_shape),
        )
    else:
        params["grid_spec"] = pltpu.PrefetchScalarGridSpec(
            num_scalar_prefetch=1,
            grid=(steps,),
            in_specs=specs,
            out_specs=out_specs or [whole(x) for x in out_shape],
        )
    return pl.pallas_call(body, **params)(scal, *args)


def stack_rows(refs, column, columns):
    return jnp.concatenate([ref[:, pl.ds(column, columns)] for ref in refs], axis=0)


def in_hbm(value):
    return pltpu.with_memory_space_constraint(value, pltpu.HBM)


def after(value, *others):
    return lax.optimization_barrier((value, *others))[0]


ROUTE_ROWS = 16


def slot_hits(cap, n, scal, route, count):
    chosen, places, _ = route
    slot = lax.broadcasted_iota(jnp.int32, (cap, count), 0)
    slot = jnp.concatenate([slot + scal[2 + j] for j in range(n)], axis=0).astype(F32)
    return slot == chosen[0] * cap + places[0], slot == chosen[1] * cap + places[1]


def token_rows(hits, tokens, back):
    hit = jnp.where(jnp.logical_or(*hits), 1.0, 0.0)
    back[...] = jnp.transpose(hit).astype(BF)
    return dot(hit.astype(BF), tokens).astype(BF)


def cotangent_rows(hits, share, cotangent):
    hit = jnp.where(jnp.logical_or(*hits), 1.0, 0.0).astype(BF)
    factor = jnp.where(hits[0], share, 0.0) + jnp.where(hits[1], 1.0 - share, 0.0)
    return (dot(hit, cotangent) * jnp.sum(factor, axis=1, keepdims=True)).astype(BF)


def own_slots_body(cap, n, scal, logits, experts, places, tokens, cotangent, *refs):
    outs, back, block = refs[:-2], refs[-2], refs[-1]
    count, width = tokens.shape
    share = jax.nn.sigmoid(logits[0:1, :] - logits[1:2, :])
    high = share.astype(BF)
    middle = (share - high.astype(F32)).astype(BF)
    low = (share - high.astype(F32) - middle.astype(F32)).astype(BF)
    chosen = experts[...].astype(F32)
    slots = places[...].astype(F32)
    rows = [chosen[0:1], chosen[1:2], slots[0:1], slots[1:2]]
    shares = [x.astype(F32) for x in (high, middle, low)]
    shares.append(jnp.zeros_like(share))
    pad = [jnp.zeros((1, width - 4 * count), F32)] if width > 4 * count else []
    head = [jnp.concatenate(x + pad, axis=1) for x in (rows, shares)]
    head.append(jnp.zeros((ROUTE_ROWS - 2, width), F32))
    block[pl.ds(0, ROUTE_ROWS), :] = jnp.concatenate(head, axis=0).astype(BF)
    block[pl.ds(ROUTE_ROWS, count), :] = tokens[...]
    route = ((chosen[0:1], chosen[1:2]), (slots[0:1], slots[1:2]), share)
    hits = slot_hits(cap, n, scal, route, count)
    rows = token_rows(hits, tokens[...], back)
    scaled = cotangent_rows(hits, share, cotangent[...])
    for j, out in enumerate(outs):
        out[:, pl.ds(0, width)] = rows[j * cap : (j + 1) * cap]
        out[:, pl.ds(width, width)] = scaled[j * cap : (j + 1) * cap]


def read_route(block, count):
    head = block[0:2, :].astype(F32)
    row = lambda r, k: head[r : r + 1, k * count : (k + 1) * count]
    share = row(1, 0) + row(1, 1) + row(1, 2)
    return (row(0, 0), row(0, 1)), (row(0, 2), row(0, 3)), share


def beside_tokens_body(cap, n, scal, block, *refs):
    outs, back = refs[:-1], refs[-1]
    count = back.shape[0]
    hits = slot_hits(cap, n, scal, read_route(block, count), count)
    rows = token_rows(hits, block[pl.ds(ROUTE_ROWS, count), :], back)
    for j, out in enumerate(outs):
        out[...] = rows[j * cap : (j + 1) * cap]


def beside_cotangents_body(cap, n, scal, block, cotangent, *outs):
    count = cotangent.shape[0]
    route = read_route(block, count)
    rows = cotangent_rows(slot_hits(cap, n, scal, route, count), route[2], cotangent[...])
    for j, out in enumerate(outs):
        out[...] = rows[j * cap : (j + 1) * cap]


def forward_body(tile, scal, *refs):
    *arrived, w_in, rows_t, hidden_t, scale_gate, scale_up = refs
    ff = w_in.shape[2] // 2
    rows = stack_rows(arrived, 0, w_in.shape[1])
    rows_t[...] = jnp.transpose(rows)
    for f in range(0, ff, tile):
        gate = dot(rows, w_in[0, :, pl.ds(f, tile)])
        upper = dot(rows, w_in[0, :, pl.ds(ff + f, tile)])
        sg = jax.nn.sigmoid(gate)
        activated = gate * sg
        hidden_t[pl.ds(f, tile), :] = jnp.transpose((activated * upper).astype(BF))
        scale_gate[:, pl.ds(f, tile)] = (upper * sg * (1.0 + gate * (1.0 - sg))).astype(BF)
        scale_up[:, pl.ds(f, tile)] = activated.astype(BF)


def core_rows(sources, offset, nz, part):
    taken = []
    for shard in range(nz):
        start = pl.multiple_of((2 * shard + offset) * part, 16)
        taken.append(jnp.concatenate([x[pl.ds(start, part), :] for x in sources], axis=1))
    return jnp.concatenate(taken, axis=0)


def shard_rows(sources, scal, nz, part):
    return jnp.concatenate(
        [core_rows(sources, offset, nz, part) for offset in (1 - scal[1], scal[1])], axis=0
    )


def pair_body(column, scal, *refs):
    *arrived, w_down, scale_gate, scale_up, pair = refs
    grad_hidden = dot_nt(stack_rows(arrived, column, w_down.shape[2]), w_down[0])
    ff = scale_gate.shape[1]
    pair[:, pl.ds(0, ff)] = (grad_hidden * scale_gate[...].astype(F32)).astype(BF)
    pair[:, pl.ds(ff, ff)] = (grad_hidden * scale_up[...].astype(F32)).astype(BF)


def put_shards(result, nz, part, before, give, keep):
    for k in range(nz):
        for out, earlier, first in ((give, before[:1], k), (keep, before[1:], nz + k)):
            total = result[first * part : (first + 1) * part]
            for x in earlier:
                total = total + x[k].astype(F32)
            out[k] = total.astype(BF)


def down_body(n, nz, other, scal, *refs):
    arrived, (hidden_a, hidden_b, out) = refs[: 2 * n], refs[2 * n :]
    part, width = out.shape[1:]
    slots = [stack_rows(arrived[:n], width, width), stack_rows(arrived[n:], 0, width)]
    offset = 1 - scal[1] if other else scal[1]
    left = core_rows((hidden_a, hidden_b), offset, nz, part)
    result = dot(left, jnp.concatenate(slots, axis=0)).astype(BF)
    for k in range(nz):
        out[k] = result[k * part : (k + 1) * part]


def input_weight_body(nz, scal, rows, pair, *refs):
    before, (give, keep) = refs[:-2], refs[-2:]
    part = give.shape[1]
    left = shard_rows((rows,), scal, nz, part)
    put_shards(dot(left, pair[...]), nz, part, before, give, keep)


def in_blocks(rows, width, columns):
    blocks = [(c, width, 0, rows, c // width * rows, 0) for c in range(0, columns - width + 1, width)]
    rest = columns % width
    first = columns - rest
    count = rest * rows // width
    for k in range(width // rest if rest else 0):
        blocks.append((first, rest, k * count, count, first // width * rows, k * rest))
    return blocks


def pack_body(scal, keep_down, other_down, *refs):
    ins, out = refs[:-1], refs[-1]
    width = keep_down.shape[2]
    top = keep_down.shape[1]
    rows = ins[0].shape[1]
    out[0, pl.ds(0, top), :] = keep_down[0] + other_down[0]
    total = jnp.concatenate([x[0] + y[0] for x, y in zip(ins[::2], ins[1::2])], axis=1)
    for c, columns, r, count, place, column in in_blocks(rows, width, total.shape[1]):
        out[0, pl.ds(top + place, count), pl.ds(column, columns)] = total[
            r : r + count, c : c + columns
        ]


def unpack_body(scal, *refs):
    terms, (grad_in, grad_down) = refs[:-2], refs[-2:]
    top, width = grad_down.shape[1:]
    rows, columns = grad_in.shape[1:]
    total = functools.reduce(jnp.add, [x[0].astype(F32) for x in terms])
    grad_down[0] = total[:top]
    for c, some, r, count, place, column in in_blocks(rows, width, columns):
        grad_in[0, pl.ds(r, count), pl.ds(c, some)] = total[
            top + place : top + place + count, column : column + some
        ]


def returned_body(cap, scal, pair, w_in, *outs):
    returned = dot_nt(pair[...], w_in[0]).astype(BF)
    for j, out in enumerate(outs):
        out[...] = returned[j * cap : (j + 1) * cap]


def combine_body(scal, back, *refs):
    *arrived, out = refs
    out[...] = dot(back[...], stack_rows(arrived, 0, out.shape[1])).astype(BF)


def per_device(tokens, cotangent, route_logits, expert_ids, slot_pos, w_in, w_down):
    token_count, width = tokens.shape
    experts, ff = w_down.shape[:2]
    n = lax.axis_size("expert")
    ndp = lax.axis_size("dp")
    nz = ndp // 2
    cap = 2 * TOP * token_count // (experts * n)
    slots = n * cap
    column, place = lax.axis_index("expert"), lax.axis_index("dp")
    z, core = place // 2, place % 2
    expert_of = lambda k: (k ^ (k >> 1)) & 1
    mine = expert_of(z)
    scal = [mine, core]
    scal += [((column ^ j) * experts + mine) * cap for j in range(n)]
    scal += [z ^ k for k in range(nz)]
    scal = jnp.stack(scal).astype(jnp.int32)
    swap_core = lambda x: lax.ppermute(x, "dp", [(i, i ^ 1) for i in range(ndp)])
    along_z = lambda x, k: lax.ppermute(x, "dp", [(i, i ^ (2 * k)) for i in range(ndp)]) if k else x
    across = lambda x, j: lax.ppermute(x, "expert", [(i, i ^ j) for i in range(n)]) if j else x
    same_core = [list(range(c, ndp, 2)) for c in range(2)]
    macs = 2 * slots * width * ff

    count = token_count
    held = [in_hbm(x) for x in (route_logits.T, expert_ids.T, slot_pos.T, tokens, cotangent)]
    *sent, back, block = call(
        functools.partial(own_slots_body, cap, n),
        [bf(cap, 2 * width)] * n + [bf(count, slots), bf(ROUTE_ROWS + count, width)],
        macs // 4,
        LIMITS[0],
        scal,
        *held,
        specs=[whole(x) for x in held],
    )
    arrived = [[across(x, j) for j, x in enumerate(sent)]]
    block = along_z(block, 1)
    cotangent = along_z(cotangent, 1)
    *sent, back_beside = call(
        functools.partial(beside_tokens_body, cap, n),
        [bf(cap, width)] * n + [bf(count, slots)],
        macs // 8,
        LIMITS[0],
        scal,
        block,
    )
    scaled = call(
        functools.partial(beside_cotangents_body, cap, n),
        [bf(cap, width)] * n,
        macs // 8,
        LIMITS[0],
        scal,
        block,
        cotangent,
    )
    arrived.append([across(x, j) for x_all in (sent, scaled) for j, x in enumerate(x_all)])
    backs = [back, back_beside]

    forwards = []
    for g in range(2):
        pieces = arrived[g][:n]
        forwards.append(
            call(
                functools.partial(forward_body, 256),
                [bf(width, slots), bf(ff, slots), bf(slots, ff), bf(slots, ff)],
                2 * macs,
                LIMITS[1],
                scal,
                *pieces,
                w_in,
                specs=[whole(x) for x in pieces] + [of_expert(w_in)],
            )
        )
    (rows_a, hidden_a, *scales_a), (rows_b, hidden_b, *scales_b) = forwards

    pairs = []
    for g, (column, scales) in enumerate(((width, scales_a), (0, scales_b))):
        pieces = arrived[g][-n:]
        if g == 0:
            pieces = [after(pieces[0], scaled[0])] + pieces[1:]
        args = pieces + [w_down] + scales
        pairs += call(
            functools.partial(pair_body, column),
            [bf(slots, 2 * ff)],
            macs,
            LIMITS[2],
            scal,
            *args,
            specs=[whole(x) for x in pieces] + [of_expert(w_down)] + [whole(x) for x in scales],
        )

    ins = []
    for rows, pair in zip((rows_a, rows_b), pairs):
        ins = call(
            functools.partial(input_weight_body, nz),
            [bf(nz, width // ndp, 2 * ff)] * 2,
            2 * macs,
            LIMITS[3],
            scal,
            rows,
            pair,
            *ins,
        )
    downs = [
        call(
            functools.partial(down_body, n, nz, other),
            [bf(nz, ff // ndp, width)],
            macs,
            LIMITS[2],
            scal,
            *arrived[0],
            *arrived[1][n:],
            hidden_a,
            hidden_b,
        )[0]
        for other in (1, 0)
    ]
    terms = [downs[1], swap_core(downs[0]), ins[1], swap_core(ins[0])]
    returned = [
        call(
            functools.partial(returned_body, cap),
            [bf(cap, width)] * n,
            2 * macs,
            LIMITS[4],
            scal,
            pair,
            w_in,
            specs=[whole(pair), of_expert(w_in)],
        )
        for pair in pairs
    ]
    rows = ff // ndp + width // ndp * 2 * ff // width
    by_z = lambda x: pl.BlockSpec((1,) + x.shape[1:], lambda k, scal: (k, 0, 0))
    packed = bf(nz, rows, width)
    (total,) = call(
        pack_body,
        [packed],
        1,
        LIMITS[6],
        scal,
        *terms,
        specs=[by_z(x) for x in terms],
        out_specs=[by_z(packed)],
        steps=nz,
    )
    total = lax.all_to_all(total, "dp", 0, 0, tiled=True, axis_index_groups=same_core)
    sets = [[k for k in range(nz) if expert_of(k) == e] for e in range(experts)]
    members = jnp.array(sets, jnp.int32).reshape(-1)
    many = len(sets[0])
    by_expert = lambda *shape: pl.BlockSpec((1,) + shape, lambda e, scal: (e, 0, 0))
    grad_in, grad_down = call(
        unpack_body,
        [
            jax.ShapeDtypeStruct((experts, width // ndp, 2 * ff), F32),
            jax.ShapeDtypeStruct((experts, ff // ndp, width), F32),
        ],
        1,
        LIMITS[6],
        members,
        *[total] * many,
        specs=[
            pl.BlockSpec((1,) + total.shape[1:], lambda e, scal, m=m: (scal[e * many + m], 0, 0))
            for m in range(many)
        ],
        out_specs=[by_expert(width // ndp, 2 * ff), by_expert(ff // ndp, width)],
        steps=experts,
    )
    sums = []
    for sent, back in zip(returned, backs):
        arrived = [across(x, j) for j, x in enumerate(sent)]
        sums += call(combine_body, [bf(count, width)], macs // 8, LIMITS[5], scal, back, *arrived)
    mine_sum, beside_sum = sums
    input_grad = (mine_sum.astype(F32) + along_z(beside_sum, 1).astype(F32)).astype(BF)
    return (input_grad, grad_in, grad_down)


LIMITS = (16, 20, 20, 20, 20, 12, 20)


def solution(mesh):
    in_specs = (
        P(("dp", "expert"), None),
        P(("dp", "expert"), None),
        P(("dp", "expert"), None),
        P(("dp", "expert"), None),
        P(("dp", "expert"), None),
        P("expert", None, None),
        P("expert", None, None),
    )
    out_specs = (P(("dp", "expert"), None), P("expert", "dp", None), P("expert", "dp", None))
    return jax.shard_map(
        per_device, mesh=mesh, in_specs=in_specs, out_specs=out_specs, check_vma=False
    )
```
